256 devices in a mesh: batch: 32 (over z, y_lo, core), tensor: 8 (over x, y_hi).
Axes of the slice: x: 4, y: 4 (y_hi: 2, y_lo: 2; y = y_hi * 2 + y_lo), z: 8, core: 2. Of those that a mesh axis runs over, the one named last changes fastest.
Arguments:
- hidden: bfloat16 [4096, 8192], P('batch'), may hold values from -6 to 6
- encodings: bfloat16 [16384, 2048], P('batch', 'tensor'), may hold values from -6 to 6
- span_slot: int32 [64], replicated, may hold values from 0 to 63, as said below
- w_query: bfloat16 [8192, 4096], P('batch', 'tensor'), may hold values from -0.0625 to 0.0625
- w_out: bfloat16 [8192, 4096], P('batch', 'tensor'), may hold values from -0.09375 to 0.09375
- w_keyval: bfloat16 [2, 2048, 4096], P(None, None, 'tensor'), may hold values from -0.125 to 0.125
- grad_out: bfloat16 [4096, 8192], P('batch'), may hold values from -6 to 6
Outputs:
- layer_out: bfloat16 [4096, 8192], P('batch', 'tensor')
- grad_hidden: bfloat16 [4096, 8192], P('batch', 'tensor')
The draws below stay inside these ranges and needn't reach their ends.
Inputs may be any that keep to these rules, and one draw needn't show every extreme that they name: span_slot is a permutation of the 64 slots; slot s lies in the rows of batch index s // 2 of encodings; the two spans of one batch index have their slots on two different batch indices, and the two slots of one batch index belong to spans of two different batch indices.
All inputs are finite; a program needn't handle non-finite values.
Results may differ from the reference program's by a relative error of at most 0.014.
Values may be sent and summed in bfloat16 or wider, within the bound.
No kernel may reach another device: no remote copies, remote signals or barrier semaphores. Data moves between devices by JAX's collectives and lax.ppermute only.
A program may use at most 128 MiB of HBM per device.

```python
import math
import jax
import jax.numpy as jnp
from jax import lax

D = 8192
HEADS = 32
HEAD = 128
DE = 2048
CL = 64
SPANS = 64
HQ = 4096
NR = 256
N_TENSOR = 8


def draw_span_slot(key, part):
    key = jax.random.fold_in(key, 11)
    owners = SPANS // 2
    key_order, key_shift, key_flip = jax.random.split(key, 3)
    order = jax.random.permutation(key_order, owners)
    shift_by = jax.random.randint(key_shift, (), 1, owners)
    flipped = jax.random.randint(key_flip, (owners,), 0, 2)
    inverse = jnp.argsort(order, stable=True).astype(jnp.int32)
    first_owner = inverse
    second_owner = (inverse - shift_by) % owners
    slot_first = 2 * first_owner
    slot_second = 2 * second_owner + 1
    span_zero = jnp.where(flipped == 0, slot_first, slot_second)
    span_one = jnp.where(flipped == 0, slot_second, slot_first)
    return jnp.stack([span_zero, span_one], axis=1).reshape(SPANS).astype(jnp.int32)


def block_levels(own_key, dims, cuts, least, largest):
    loudness, own = 1.0, jax.random.fold_in(own_key, 6)
    for position, shards_of in cuts:
        steps = jnp.exp(jax.random.uniform(jax.random.fold_in(own, position), (shards_of,), jnp.float32, least / len(cuts), largest / len(cuts)))
        loudness = loudness * jnp.repeat(steps, dims[position] // shards_of).reshape([-1 if axis == position else 1 for axis in range(len(dims))])
    return loudness


def normal_values(own_key, shape, scale, bound, shards=(), kind=jnp.bfloat16):
    gain = block_levels(own_key, shape, shards, -0.22, 0.18) if shards else 1.0
    values = jax.random.normal(own_key, shape, jnp.float32) * scale * gain
    return jnp.minimum(jnp.maximum(values, -bound), bound).astype(kind)


def setup_inputs(seed: int = 0) -> dict:
    key_of = jax.random.split(jax.random.key(seed), 8)
    return {
        "hidden": normal_values(key_of[0], (SPANS * CL, D), 1.0, 6.0, ((0, 32),)),
        "encodings": normal_values(key_of[1], (SPANS * NR, DE), 1.0, 6.0, ((0, 32), (1, 8))),
        "span_slot": draw_span_slot(jax.random.fold_in(key_of[7], 71), 0),
        "w_query": normal_values(key_of[3], (D, HQ), D ** -0.5, 0.0625, ((0, 32), (1, 8))),
        "w_out": normal_values(key_of[4], (D, HQ), HQ ** -0.5, 0.09375, ((0, 32), (1, 8))),
        "w_keyval": normal_values(key_of[5], (2, DE, HQ), DE ** -0.5, 0.125, ((2, 8),)),
        "grad_out": normal_values(key_of[6], (SPANS * CL, D), 1.0, 6.0, ((0, 32),)),
    }


def grouped_product(left_side, right_side):
    group_cols = HQ // N_TENSOR
    running = jnp.zeros((left_side.shape[0], right_side.shape[0]), jnp.float32)
    for group_idx in range(N_TENSOR):
        lower = group_idx * group_cols
        upper = lower + group_cols
        piece_sum = jnp.dot(left_side[:, lower:upper], right_side[:, lower:upper].T, preferred_element_type=jnp.float32)
        running = running + piece_sum.astype(jnp.bfloat16).astype(jnp.float32)
    return running

def reference(hidden, encodings, span_slot, w_query, w_out, w_keyval, grad_out):
    scaling = 1.0 / math.sqrt(HEAD)
    slot_blocks = encodings.reshape(SPANS, NR, DE)
    enc_rows = jnp.take(slot_blocks, span_slot.astype(jnp.int32), axis=0).reshape(SPANS * NR, DE)
    query_rows = (jnp.dot(hidden, w_query, preferred_element_type=jnp.float32) * scaling).astype(jnp.bfloat16)
    key_rows = jnp.dot(enc_rows, w_keyval[0], preferred_element_type=jnp.float32).astype(jnp.bfloat16)
    value_rows = jnp.dot(enc_rows, w_keyval[1], preferred_element_type=jnp.float32).astype(jnp.bfloat16)
    query_heads = query_rows.astype(jnp.float32).reshape(SPANS, CL, HEADS, HEAD)
    key_heads = key_rows.astype(jnp.float32).reshape(SPANS, NR, HEADS, HEAD)
    value_heads = value_rows.astype(jnp.float32).reshape(SPANS, NR, HEADS, HEAD)
    scores = jnp.einsum('cqhe,ckhe->chqk', query_heads, key_heads)
    probs = jax.nn.softmax(scores, axis=-1)
    probs_bf = probs.astype(jnp.bfloat16)
    attended = jnp.einsum('chqk,ckhe->cqhe', probs_bf.astype(jnp.float32), value_heads).astype(jnp.bfloat16)
    attended_rows = attended.reshape(SPANS * CL, HQ)
    layer_out = (hidden.astype(jnp.float32) + grouped_product(attended_rows, w_out)).astype(jnp.bfloat16)
    grad_attended = jnp.dot(grad_out, w_out, preferred_element_type=jnp.float32).astype(jnp.bfloat16)
    grad_heads = grad_attended.astype(jnp.float32).reshape(SPANS, CL, HEADS, HEAD)
    row_delta = lax.optimization_barrier(jnp.sum(grad_heads * attended.astype(jnp.float32), axis=-1))
    row_delta = jnp.transpose(row_delta, (0, 2, 1))
    grad_probs = jnp.einsum('cqhe,ckhe->chqk', grad_heads, value_heads)
    grad_scores = (probs * (grad_probs - row_delta[..., None])).astype(jnp.bfloat16)
    grad_query = (jnp.einsum('chqk,ckhe->cqhe', grad_scores.astype(jnp.float32), key_heads) * scaling).astype(jnp.bfloat16)
    grad_query = grad_query.reshape(SPANS * CL, HQ)
    grad_hidden = (grad_out.astype(jnp.float32) + grouped_product(grad_query, w_query)).astype(jnp.bfloat16)
    return (layer_out, grad_hidden)
```

```python
import math

import jax
import jax.numpy as jnp
from jax import lax
from jax.sharding import PartitionSpec as P

HEAD = 128
CL = 64
NR = 256
Z = 8
X = 4
BF16 = jnp.bfloat16
F32 = jnp.float32


def along_z(a, step):
    return lax.ppermute(a, "batch", [(i, (i + 4 * step) % 32) for i in range(32)])


def swap_y(a):
    return lax.ppermute(a, "batch", [(i, i ^ 2) for i in range(32)])


def swap_core(a):
    return lax.ppermute(a, "batch", [(i, i ^ 1) for i in range(32)])


def along_x(a, step):
    return lax.ppermute(a, "tensor", [(i, (i + 2 * step) % 8) for i in range(8)])


def swap_far_y(a):
    return lax.ppermute(a, "tensor", [(i, i ^ 1) for i in range(8)])


def pick(a, index):
    return lax.dynamic_index_in_dim(a, index, 0, keepdims=False)


def flip_if(a, axis, yes):
    return jnp.where(yes, jnp.flip(a, axis), a)


def gather_weights(w_query, w_out):
    own = jnp.stack([w_query, w_out])
    half = own.shape[1] // 2
    other = swap_y(own[:, :half])
    blocks = [None] * Z
    start = jnp.concatenate([own, other], axis=1)
    blocks[0] = start
    ahead = jnp.concatenate([along_z(own, -1), along_z(other, -1)], axis=1)
    back = jnp.concatenate([along_z(own, 1), along_z(other, 1)], axis=1)
    for step in range(1, Z // 2):
        blocks[step] = ahead
        blocks[Z - step] = back
        if step < Z // 2 - 1:
            ahead, back = along_z(ahead, -1), along_z(back, 1)
    cols = own.shape[2] // 2
    left = along_z(ahead[:, :, :cols], -1)
    right = along_z(back[:, :, cols:], 1)
    blocks[Z // 2] = jnp.concatenate([left, right], axis=2)
    out = []
    for block in blocks:
        late = swap_y(block[:, half : 2 * half])
        mine = jnp.concatenate([block, late], axis=1)
        theirs = swap_core(mine)
        out.append((mine, theirs))
    full = []
    for w in range(2):
        rows = [part[w] for pair in out for part in pair]
        full.append(jnp.concatenate(rows, axis=0))
    return full


def relative_columns(a, z, y_lo, core):
    rows = a.shape[0]
    a = a.reshape(rows, Z, 2, 2, a.shape[1] // (4 * Z))
    twice = jnp.concatenate([a, a], axis=1)
    a = lax.dynamic_slice_in_dim(twice, z, Z, 1)
    a = flip_if(flip_if(a, 2, y_lo == 1), 3, core == 1)
    return jnp.transpose(a, (0, 1, 3, 2, 4)).reshape(rows, -1)


def route(encodings, span_slot):
    owners = 32
    slots = encodings.shape[0] // NR
    width = encodings.shape[1]
    piece = NR // owners
    spread = encodings.reshape(slots, owners, piece, width).transpose(1, 0, 2, 3)
    spread = lax.all_to_all(spread, "batch", 0, 0)
    spread = spread.reshape(owners * slots, piece, width)
    count = span_slot.shape[0]
    matches = (span_slot[:, None] == jnp.arange(count, dtype=jnp.int32)[None, :]).astype(BF16)
    chosen = jnp.einsum("cs,srw->crw", matches, spread, preferred_element_type=F32).astype(BF16)
    chosen = chosen.reshape(owners, count // owners, piece, width)
    chosen = lax.all_to_all(chosen, "batch", 0, 0)
    return chosen.transpose(1, 0, 2, 3).reshape(count // owners * NR, width)


def gather_features(enc):
    half = enc.shape[0] // 2

    def ring(a):
        left, right = along_x(a, 1), along_x(a, -1)
        far = jnp.concatenate([along_x(left[:half], 1), along_x(right[half:], -1)], axis=0)
        return [a, left, far, right]

    return jnp.concatenate(ring(enc) + ring(swap_far_y(enc)), axis=1)


def relative_rows(w, x, y_hi):
    kinds, depth, cols = w.shape
    w = w.reshape(kinds, X, 2, depth // 8, cols)
    w = jnp.flip(w, 1)
    twice = jnp.concatenate([w, w], axis=1)
    w = lax.dynamic_slice_in_dim(twice, X - 1 - x, X, 1)
    w = flip_if(w, 2, y_hi == 1)
    return jnp.transpose(w, (0, 2, 1, 3, 4)).reshape(kinds, depth, cols)


def summed(left_side, weights, z, x, y_hi):
    tokens = left_side.shape[0]
    weights = weights.reshape(Z, -1, weights.shape[1])

    def part(dx):
        out = []
        for dy in range(2):
            target = lax.rem(x + dx + X, X) * 2 + (y_hi ^ dy)
            block = pick(weights, lax.rem(target - z + Z, Z))
            out.append(
                lax.dot_general(
                    left_side, block, (((1,), (1,)), ((), ())), preferred_element_type=F32
                ).astype(BF16)
            )
        return jnp.stack(out)

    half = tokens // 2
    far = part(2)
    from_left = along_x(far[:, :half], 1)
    from_right = along_x(far[:, half:], -1)
    after, before = part(1), part(-1)
    after = jnp.concatenate([after[:, :half] + from_left, after[:, half:]], axis=1)
    before = jnp.concatenate([before[:, :half], before[:, half:] + from_right], axis=1)
    got_left = along_x(after, 1)
    got_right = along_x(before, -1)
    total = part(0).astype(F32) + got_left.astype(F32) + got_right.astype(F32)
    other = swap_far_y(total[1].astype(BF16))
    return total[0] + other.astype(F32)


def attend(query_heads, key_heads, value_heads):
    scores = jnp.einsum("cqhe,ckhe->chqk", query_heads, key_heads, preferred_element_type=F32)
    probs = jax.nn.softmax(scores, axis=-1)
    combined = jnp.einsum(
        "chqk,ckhe->cqhe", probs.astype(BF16), value_heads, preferred_element_type=F32
    )
    return (probs, combined.astype(BF16))


def shards(hidden, encodings, span_slot, w_query, w_out, w_keyval, grad_out):
    scaling = 1.0 / math.sqrt(HEAD)
    tokens = hidden.shape[0]
    span_dev = tokens // CL
    local_cols = w_query.shape[1]
    head_count = local_cols // HEAD
    batch = lax.axis_index("batch")
    tensor = lax.axis_index("tensor")
    z, y_lo, core = batch // 4, batch // 2 % 2, batch % 2
    x, y_hi = tensor // 2, tensor % 2

    enc = route(encodings, span_slot)
    query_full, out_full = gather_weights(w_query, w_out)
    full_enc = gather_features(enc)
    w_kv = relative_rows(w_keyval, x, y_hi)

    hidden_rel = relative_columns(hidden, z, y_lo, core)
    grad_rel = relative_columns(grad_out, z, y_lo, core)
    query = (jnp.dot(hidden_rel, query_full, preferred_element_type=F32) * scaling).astype(BF16)
    query_heads = query.reshape(span_dev, CL, head_count, HEAD)
    keys = jnp.dot(full_enc, w_kv[0], preferred_element_type=F32).astype(BF16)
    key_heads = keys.reshape(span_dev, NR, head_count, HEAD)
    values = jnp.dot(full_enc, w_kv[1], preferred_element_type=F32).astype(BF16)
    value_heads = values.reshape(span_dev, NR, head_count, HEAD)
    probs, attended = attend(query_heads, key_heads, value_heads)
    mixed_sum = summed(attended.reshape(tokens, local_cols), out_full, z, x, y_hi)

    grad_attended = jnp.dot(grad_rel, out_full, preferred_element_type=F32).astype(BF16)
    grad_attended = grad_attended.reshape(span_dev, CL, head_count, HEAD)
    row_delta = jnp.sum(grad_attended.astype(F32) * attended.astype(F32), axis=-1)
    row_delta = jnp.transpose(row_delta, (0, 2, 1))
    grad_probs = jnp.einsum(
        "cqhe,ckhe->chqk", grad_attended, value_heads, preferred_element_type=F32
    )
    grad_scores = (probs * (grad_probs - row_delta[..., None])).astype(BF16)
    grad_query = jnp.einsum(
        "chqk,ckhe->cqhe", grad_scores, key_heads, preferred_element_type=F32
    )
    grad_query = (grad_query * scaling).astype(BF16).reshape(tokens, local_cols)
    back_sum = summed(grad_query, query_full, z, x, y_hi)

    def finish(base, total):
        cols = total.shape[1]
        own = lax.dynamic_slice_in_dim(base, tensor * cols, cols, 1)
        total = total.reshape(tokens, 2, 2, cols // 4)
        total = flip_if(flip_if(total, 1, core == 1), 2, y_lo == 1)
        total = jnp.transpose(total, (0, 2, 1, 3)).reshape(tokens, cols)
        return (own.astype(F32) + total).astype(BF16)

    return (finish(hidden, mixed_sum), finish(grad_out, back_sum))


def solution(mesh):
    return jax.shard_map(
        shards,
        mesh=mesh,
        in_specs=(
            P("batch", None),
            P("batch", "tensor"),
            P(),
            P("batch", "tensor"),
            P("batch", "tensor"),
            P(None, None, "tensor"),
            P("batch", None),
        ),
        out_specs=(P("batch", "tensor"), P("batch", "tensor")),
        check_vma=False,
    )
```

```python
import functools
import math

import jax
import jax.numpy as jnp
from jax import lax
from jax.experimental import pallas as pl
from jax.experimental.pallas import tpu as pltpu
from jax.sharding import PartitionSpec as P

HEAD = 128
CL = 64
NR = 256
Z = 8
BF16 = jnp.bfloat16
F32 = jnp.float32
MIB = 1 << 20


def along_z(a, step):
    return lax.ppermute(a, "batch", [(i, (i + 4 * step) % 32) for i in range(32)])


def swap_core(a):
    return lax.ppermute(a, "batch", [(i, i ^ 1) for i in range(32)])


def swap_y(a):
    return lax.ppermute(a, "batch", [(i, i ^ 2) for i in range(32)])


def swap_far_y(a):
    return lax.ppermute(a, "tensor", [(i, i ^ 1) for i in range(8)])


def swap_other_y(a):
    pairs = [(b * 8 + t, (b ^ 2) * 8 + (t ^ 1)) for b in range(32) for t in range(8)]
    return lax.ppermute(a, ("batch", "tensor"), pairs)


def along_x(a, step):
    return lax.ppermute(a, "tensor", [(i, (i + 2 * step) % 8) for i in range(8)])


def dot(a, b):
    return jnp.dot(a, b, preferred_element_type=F32)


def dot_t(a, b):
    return lax.dot_general(a, b, (((1,), (1,)), ((), ())), preferred_element_type=F32)


SMEM = pl.BlockSpec(memory_space=pltpu.SMEM)
VMEM = pl.BlockSpec(memory_space=pltpu.VMEM)


def call(kernel, outs, ins, specs=None, flops=0, limit=32, scratch=(), grid=()):
    size = sum(math.prod(a.shape) * a.dtype.itemsize for a in list(ins) + list(outs))
    return pl.pallas_call(
        kernel,
        out_shape=outs,
        in_specs=specs or [SMEM] + [VMEM] * (len(ins) - 1),
        out_specs=[VMEM] * len(outs),
        scratch_shapes=list(scratch),
        grid=grid,
        compiler_params=pltpu.CompilerParams(vmem_limit_bytes=limit * MIB),
        cost_estimate=pl.CostEstimate(flops=flops, bytes_accessed=size, transcendentals=0),
    )(*ins)


def shape(*dims, kind=BF16):
    return jax.ShapeDtypeStruct(dims, kind)


def aligned(offset, size):
    return pl.ds(pl.multiple_of(offset, size), size)


def spread_kernel(enc, out):
    for slot in range(2):
        for rows in range(16):
            for cols in range(2):
                out[rows * 2 + cols, slot] = enc[
                    slot * NR + rows * 16 : slot * NR + rows * 16 + 16,
                    cols * 128 : cols * 128 + 128,
                ]


def choose_kernel(slots, pieces, out):
    for span in range(64):
        out[span // 2, span % 2] = pieces[slots[span]]


def assemble_kernel(pieces, out):
    for span in range(2):
        for rows in range(16):
            for cols in range(2):
                out[
                    span * NR + rows * 16 : span * NR + rows * 16 + 16,
                    cols * 128 : cols * 128 + 128,
                ] = pieces[rows * 2 + cols, span]


def route(encodings, span_slot):
    spread = call(spread_kernel, [shape(32, 2, 16, 128)], [encodings], [VMEM])[0]
    spread = lax.all_to_all(spread, "batch", 0, 0).reshape(64, 16, 128)
    chosen = call(choose_kernel, [shape(32, 2, 16, 128)], [span_slot, spread])[0]
    chosen = lax.all_to_all(chosen, "batch", 0, 0)
    return call(assemble_kernel, [shape(512, 256)], [chosen], [VMEM])[0]


def gather_features(enc):
    other = swap_far_y(enc)
    pieces = [(0, 0, enc), (0, 1, other)]
    for dy, piece in ((0, enc), (1, other)):
        for dx in (1, -1, 2):
            pieces.append((dx, dy, along_x(piece, dx)))
    return pieces


def keyval_kernel(places, meta, w, *refs):
    pieces, (keys, values) = refs[:-2], refs[-2:]
    x, y_hi = meta[3], meta[4]
    for kind, out in ((0, keys), (1, values)):
        total = None
        for (dx, dy), piece in zip(places, pieces):
            source = ((x - dx) & 3) * 2 + (y_hi ^ dy)
            term = dot(piece[...], w[kind, aligned(source * 256, 256), :])
            total = term if total is None else total + term
        out[...] = total.astype(BF16)


def half_kernel(meta, hidden, grad, out_hidden, out_grad):
    y_lo = meta[1]
    for source, out in ((hidden, out_hidden), (grad, out_grad)):
        for block in range(Z):
            out[block] = source[:, aligned(block * 1024 + (1 - y_lo) * 512, 512)]


def ring_weights(w_query, w_out):
    own = jnp.stack([w_query, w_out])
    blocks = {0: own}
    ahead = back = own
    for step in range(1, Z // 2):
        ahead, back = along_z(ahead, -1), along_z(back, 1)
        blocks[step], blocks[Z - step] = ahead, back
    last = [along_z(ahead[0], -1), along_z(back[1], 1)]
    found = {}
    for step, block in blocks.items():
        theirs = swap_core(block)
        for w in range(2):
            found[step, w, 0], found[step, w, 1] = (block, w), (theirs, w)
    for w in range(2):
        found[Z // 2, w, 0], found[Z // 2, w, 1] = (last[w], None), (swap_core(last[w]), None)
    return found


def one_block(array, index):
    if index is None:
        return pl.BlockSpec(array.shape, lambda i: (0, 0))
    return pl.BlockSpec((None,) + array.shape[1:], lambda i: (index, 0, 0))


def project_kernel(keys, places, first, last, meta, hidden, grad, hidden_in, grad_in, *refs):
    z, y_lo, core = meta[0], meta[1], meta[2]
    refs = list(refs)
    before = None if first else refs.pop(0)
    outs = refs[len(refs) - 1 - last :]
    for w, (own, arrived) in enumerate(((hidden, hidden_in), (grad, grad_in))):
        total = None if first else before[w]
        for step, kind, apart in keys:
            if kind != w:
                continue
            place, side = (z + step) & 7, core ^ apart
            left = jnp.concatenate(
                [
                    own[:, aligned(place * 1024 + y_lo * 512 + side * 256, 256)],
                    arrived[place, :, aligned(side * 256, 256)],
                ],
                axis=0,
            )
            number, index = places[step, kind, apart]
            block = refs[number][...] if index is None else refs[number][index]
            term = dot(left, block)
            total = term if total is None else total + term
        if last:
            outs[0][w] = total[:128]
            outs[1][w] = total[128:].astype(BF16)
        else:
            outs[0][w] = total


def project(steps, meta, acts, found, before=None, last=False):
    keys = [(s, w, c) for s in steps for w in range(2) for c in range(2)]
    arrays, places = [], {}
    for key in keys:
        array, index = found[key]
        number = next((n for n, a in enumerate(arrays) if a is array), len(arrays))
        if number == len(arrays):
            arrays.append(array)
        places[key] = (number, index)
    ins = [meta, *acts] + ([] if before is None else [before]) + arrays
    if last:
        outs = [shape(2, 128, 512, kind=F32), shape(2, 128, 512)]
    else:
        outs = [shape(2, 256, 512, kind=F32)]
    kernel = functools.partial(project_kernel, keys, places, before is None, last)
    return call(kernel, outs, ins, flops=len(keys) * 2 * 256 * 256 * 512)


def attend_kernel(own, arrived, keys, values, attended, grad_query):
    scaling = 1.0 / math.sqrt(HEAD)
    query = ((own[0] + arrived[0].astype(F32)) * scaling).astype(BF16)
    grad = (own[1] + arrived[1].astype(F32)).astype(BF16)
    for span in range(2):
        rows = slice(span * CL, span * CL + CL)
        for head in range(4):
            cols = slice(head * HEAD, head * HEAD + HEAD)
            k = keys[span * NR : span * NR + NR, cols]
            v = values[span * NR : span * NR + NR, cols]
            scores = dot_t(query[rows, cols], k)
            top = jnp.max(scores, axis=-1, keepdims=True)
            powers = jnp.exp(scores - top)
            probs = powers / jnp.sum(powers, axis=-1, keepdims=True)
            out = dot(probs.astype(BF16), v).astype(BF16)
            attended[rows, cols] = out
            g = grad[rows, cols]
            delta = jnp.sum(g.astype(F32) * out.astype(F32), axis=-1, keepdims=True)
            grad_scores = (probs * (dot_t(g, v) - delta)).astype(BF16)
            grad_query[rows, cols] = (dot(grad_scores, k) * scaling).astype(BF16)


def expand_kernel(keys, meta, own, arrived, *refs):
    z, core, x, y_hi = meta[0], meta[2], meta[3], meta[4]
    blocks = refs[: len(keys)]
    far0, far1, plus0, plus1, minus0, minus1, here, placed = refs[len(keys) :]
    left = jnp.concatenate([own[...], arrived[...]], axis=0)
    for (step, _, apart), block in zip(keys, blocks):
        target = (z + step) & 7
        dx, dy = ((target >> 1) - x) & 3, (target & 1) ^ y_hi
        side = aligned((core ^ apart) * 256, 256)
        part = dot_t(left, block[...]).astype(BF16)
        placed[dx, 0, dy, :, side] = part[:128]
        placed[dx, 1, dy, :, side] = part[128:]
    here[...] = placed[0]
    plus0[...], plus1[...] = placed[1, 0], placed[1, 1]
    far0[...], far1[...] = placed[2, 0], placed[2, 1]
    minus0[...], minus1[...] = placed[3, 0], placed[3, 1]


def add_kernel(a, b, c, d, ab, cd):
    ab[...] = (a[...].astype(F32) + b[...].astype(F32)).astype(BF16)
    cd[...] = (c[...].astype(F32) + d[...].astype(F32)).astype(BF16)


def total_kernel(here, left0, left1, right0, right1, keep, across, near, cross):
    own = here[0].astype(F32) + left0[...].astype(F32) + right0[...].astype(F32)
    keep[...] = own[0]
    across[...] = own[1].astype(BF16)
    other = here[1].astype(F32) + left1[...].astype(F32) + right1[...].astype(F32)
    near[...] = other[0].astype(BF16)
    cross[...] = other[1].astype(BF16)


def finish_kernel(meta, base, keep, across, near, cross, out):
    tensor = meta[3] * 2 + meta[4]
    y_lo = meta[1]
    mine, other = y_lo * 512, (1 - y_lo) * 512
    start = tensor * 1024
    out[:, aligned(mine, 512)] = (
        base[:, aligned(start + mine, 512)].astype(F32) + (keep[...] + across[...].astype(F32))
    ).astype(BF16)
    out[:, aligned(other, 512)] = (
        base[:, aligned(start + other, 512)].astype(F32)
        + (near[...].astype(F32) + cross[...].astype(F32))
    ).astype(BF16)


def summed(meta, left_side, w, found, base):
    arrived = swap_y(left_side)
    keys = [(s, w, c) for s in range(Z) for c in range(2)]
    arrays = [found[key][0] for key in keys]
    specs = [one_block(*found[key]) for key in keys]
    part = shape(2, 128, 512)
    far0, far1, plus0, plus1, minus0, minus1, here = call(
        functools.partial(expand_kernel, keys),
        [part] * 6 + [shape(2, 2, 128, 512)],
        [meta, left_side, arrived] + arrays,
        [SMEM, VMEM, VMEM] + specs,
        flops=2 * 256 * 512 * 4096,
        scratch=[pltpu.VMEM((4, 2, 2, 128, 512), BF16)],
        grid=(1,),
    )
    from_left, from_right = along_x(far0, 1), along_x(far1, -1)
    left1, right0 = along_x(plus1, 1), along_x(minus0, -1)
    plus0, minus1 = call(add_kernel, [part] * 2, [plus0, from_left, minus1, from_right], [VMEM] * 4)
    left0, right1 = along_x(plus0, 1), along_x(minus1, -1)
    flat = shape(128, 512)
    keep, across, near, cross = call(
        total_kernel,
        [shape(128, 512, kind=F32), flat, flat, flat],
        [here, left0, left1, right0, right1],
        [VMEM] * 5,
    )
    across, near, cross = swap_far_y(across), swap_y(near), swap_other_y(cross)
    return call(finish_kernel, [shape(128, 1024)], [meta, base, keep, across, near, cross])[0]


def shards(hidden, encodings, span_slot, w_query, w_out, w_keyval, grad_out):
    batch = lax.axis_index("batch")
    tensor = lax.axis_index("tensor")
    meta = jnp.stack([batch // 4, batch // 2 % 2, batch % 2, tensor // 2, tensor % 2]).astype(jnp.int32)

    found = ring_weights(w_query, w_out)
    enc = route(encodings, span_slot)
    half = call(half_kernel, [shape(Z, 128, 512)] * 2, [meta, hidden, grad_out])
    acts = [hidden, grad_out, swap_y(half[0]), swap_other_y(half[1])]
    pieces = gather_features(enc)
    keys, values = call(
        functools.partial(keyval_kernel, [(dx, dy) for dx, dy, _ in pieces]),
        [shape(512, 512)] * 2,
        [meta, w_keyval] + [piece for _, _, piece in pieces],
        flops=4 * 512 * 2048 * 512,
    )
    early = project((0, 1, 7, 2, 6), meta, acts, found)[0]
    own, sent = project((3, 5, 4), meta, acts, found, early, True)
    attended, grad_query = call(
        attend_kernel,
        [shape(128, 512)] * 2,
        [own, swap_y(sent), keys, values],
        [VMEM] * 4,
        flops=10 * 8 * 64 * 256 * 128,
    )
    layer_out = summed(meta, attended, 1, found, hidden)
    grad_hidden = summed(meta, grad_query, 0, found, grad_out)
    return (layer_out, grad_hidden)


def solution(mesh):
    return jax.shard_map(
        shards,
        mesh=mesh,
        in_specs=(
            P("batch", None),
            P("batch", "tensor"),
            P(),
            P("batch", "tensor"),
            P("batch", "tensor"),
            P(None, None, "tensor"),
            P("batch", None),
        ),
        out_specs=(P("batch", "tensor"), P("batch", "tensor")),
        check_vma=False,
    )
```

```python
import functools
import math

import jax
import jax.numpy as jnp
from jax import lax
from jax.experimental import pallas as pl
from jax.experimental.pallas import tpu as pltpu
from jax.sharding import PartitionSpec as P

HEAD = 128
CL = 64
NR = 256
Z = 8
BF16 = jnp.bfloat16
F32 = jnp.float32
MIB = 1 << 20


def along_z(a, step):
    return lax.ppermute(a, "batch", [(i, (i + 4 * step) % 32) for i in range(32)])


def swap_core(a):
    return lax.ppermute(a, "batch", [(i, i ^ 1) for i in range(32)])


def swap_y(a):
    return lax.ppermute(a, "batch", [(i, i ^ 2) for i in range(32)])


def swap_far_y(a):
    return lax.ppermute(a, "tensor", [(i, i ^ 1) for i in range(8)])


def swap_other_y(a):
    pairs = [(b * 8 + t, (b ^ 2) * 8 + (t ^ 1)) for b in range(32) for t in range(8)]
    return lax.ppermute(a, ("batch", "tensor"), pairs)


def along_x(a, step):
    return lax.ppermute(a, "tensor", [(i, (i + 2 * step) % 8) for i in range(8)])


def dot(a, b):
    return jnp.dot(a, b, preferred_element_type=F32)


def dot_t(a, b):
    return lax.dot_general(a, b, (((1,), (1,)), ((), ())), preferred_element_type=F32)


SMEM = pl.BlockSpec(memory_space=pltpu.SMEM)
VMEM = pl.BlockSpec(memory_space=pltpu.VMEM)


def call(kernel, outs, ins, specs=None, flops=0, limit=32, scratch=(), grid=()):
    size = sum(math.prod(a.shape) * a.dtype.itemsize for a in list(ins) + list(outs))
    return pl.pallas_call(
        kernel,
        out_shape=outs,
        in_specs=specs or [SMEM] + [VMEM] * (len(ins) - 1),
        out_specs=[VMEM] * len(outs),
        scratch_shapes=list(scratch),
        grid=grid,
        compiler_params=pltpu.CompilerParams(vmem_limit_bytes=limit * MIB),
        cost_estimate=pl.CostEstimate(flops=flops, bytes_accessed=size, transcendentals=0),
    )(*ins)


def shape(*dims, kind=BF16):
    return jax.ShapeDtypeStruct(dims, kind)


def aligned(offset, size):
    return pl.ds(pl.multiple_of(offset, size), size)


def spread_kernel(enc, out):
    for slot in range(2):
        for rows in range(16):
            for cols in range(2):
                out[rows * 2 + cols, slot] = enc[
                    slot * NR + rows * 16 : slot * NR + rows * 16 + 16,
                    cols * 128 : cols * 128 + 128,
                ]


def choose_kernel(slots, pieces, out):
    for span in range(64):
        out[span // 2, span % 2] = pieces[slots[span]]


def assemble_kernel(pieces, out):
    for span in range(2):
        for rows in range(16):
            for cols in range(2):
                out[
                    span * NR + rows * 16 : span * NR + rows * 16 + 16,
                    cols * 128 : cols * 128 + 128,
                ] = pieces[rows * 2 + cols, span]


def gather_features(enc):
    other = swap_far_y(enc)
    near = [(dx, 0, along_x(enc, dx)) for dx in (1, -1, 2)]
    return [(0, 0, enc), (0, 1, other)] + near + [(dx, 1, along_x(other, dx)) for dx in (1, -1, 2)]


def keyval_kernel(places, meta, w, *refs):
    pieces, (keys, values) = refs[:-2], refs[-2:]
    x, y_hi = meta[3], meta[4]
    for kind, out in ((0, keys), (1, values)):
        total = None
        for (dx, dy), piece in zip(places, pieces):
            source = ((x - dx) & 3) * 2 + (y_hi ^ dy)
            term = dot(piece[...], w[kind, aligned(source * 256, 256), :])
            total = term if total is None else total + term
        out[...] = total.astype(BF16)


def half_kernel(meta, hidden, grad, out_hidden, out_grad):
    y_lo = meta[1]
    for source, out in ((hidden, out_hidden), (grad, out_grad)):
        for block in range(Z):
            out[block] = source[:, aligned(block * 1024 + (1 - y_lo) * 512, 512)]


def after(value, *others):
    return lax.optimization_barrier((value, others))[0]


def along_both(ahead, back):
    return along_z(ahead, -1), along_z(back, 1)


def with_core(blocks, last):
    found = {}
    behind = {0: 2, 1: 2, 7: 2, 2: 3, 6: 3}
    for step, block in blocks.items():
        if step in behind:
            ready = after(block, blocks[behind[step]], blocks[Z - behind[step]])
        else:
            ready = block
        theirs = swap_core(ready)
        for w in range(2):
            found[step, w, 0], found[step, w, 1] = (block, w), (theirs, w)
    for w in range(2):
        found[Z // 2, w, 0], found[Z // 2, w, 1] = (last[w], None), (swap_core(last[w]), None)
    return found


def one_block(array, index):
    if index is None:
        return pl.BlockSpec(array.shape, lambda i: (0, 0))
    return pl.BlockSpec((None,) + array.shape[1:], lambda i: (index, 0, 0))


def project_kernel(keys, places, first, last, meta, hidden, grad, hidden_in, grad_in, *refs):
    z, y_lo, core = meta[0], meta[1], meta[2]
    refs = list(refs)
    before = None if first else refs.pop(0)
    outs = refs[len(refs) - 1 - last :]
    for w, (own, arrived) in enumerate(((hidden, hidden_in), (grad, grad_in))):
        total = None if first else before[w]
        for step, kind, apart in keys:
            if kind != w:
                continue
            place, side = (z + step) & 7, core ^ apart
            left = jnp.concatenate(
                [
                    own[:, aligned(place * 1024 + y_lo * 512 + side * 256, 256)],
                    arrived[place, :, aligned(side * 256, 256)],
                ],
                axis=0,
            )
            number, index = places[step, kind, apart]
            block = refs[number][...] if index is None else refs[number][index]
            term = dot(left, block)
            total = term if total is None else total + term
        if last:
            outs[0][w] = total[:128]
            outs[1][w] = total[128:].astype(BF16)
        else:
            outs[0][w] = total


def project(steps, meta, acts, found, before=None, last=False):
    keys = [(s, w, c) for s in steps for w in range(2) for c in range(2)]
    arrays, places = [], {}
    for key in keys:
        array, index = found[key]
        number = next((n for n, a in enumerate(arrays) if a is array), len(arrays))
        if number == len(arrays):
            arrays.append(array)
        places[key] = (number, index)
    ins = [meta, *acts] + ([] if before is None else [before]) + arrays
    if last:
        outs = [shape(2, 128, 512, kind=F32), shape(2, 128, 512)]
    else:
        outs = [shape(2, 256, 512, kind=F32)]
    kernel = functools.partial(project_kernel, keys, places, before is None, last)
    return call(kernel, outs, ins, flops=len(keys) * 2 * 256 * 256 * 512)


def attend_kernel(own, arrived, keys, values, both):
    scaling = 1.0 / math.sqrt(HEAD)
    query = ((own[0] + arrived[0].astype(F32)) * scaling).astype(BF16)
    grad = (own[1] + arrived[1].astype(F32)).astype(BF16)
    for span in range(2):
        rows = slice(span * CL, span * CL + CL)
        for head in range(4):
            cols = slice(head * HEAD, head * HEAD + HEAD)
            k = keys[span * NR : span * NR + NR, cols]
            v = values[span * NR : span * NR + NR, cols]
            scores = dot_t(query[rows, cols], k)
            top = jnp.max(scores, axis=-1, keepdims=True)
            powers = jnp.exp(scores - top)
            probs = powers / jnp.sum(powers, axis=-1, keepdims=True)
            out = dot(probs.astype(BF16), v).astype(BF16)
            both[0, rows, cols] = out
            g = grad[rows, cols]
            delta = jnp.sum(g.astype(F32) * out.astype(F32), axis=-1, keepdims=True)
            grad_scores = (probs * (dot_t(g, v) - delta)).astype(BF16)
            both[1, rows, cols] = (dot(grad_scores, k) * scaling).astype(BF16)


def expand_kernel(keys, kind, meta, own, arrived, *refs):
    z, core, x, y_hi = meta[0], meta[2], meta[3], meta[4]
    blocks = refs[: len(keys)]
    right, left, plus0, minus1, here, placed = refs[len(keys) :]
    rows = jnp.concatenate([own[kind], arrived[kind]], axis=0)
    for (step, _, apart), block in zip(keys, blocks):
        target = (z + step) & 7
        dx, dy = ((target >> 1) - x) & 3, (target & 1) ^ y_hi
        side = aligned((core ^ apart) * 256, 256)
        part = dot_t(rows, block[...]).astype(BF16)
        placed[dx, 0, dy, :, side] = part[:128]
        placed[dx, 1, dy, :, side] = part[128:]
    here[...] = placed[0]
    right[0], right[1] = placed[2, 0], placed[1, 1]
    left[0], left[1] = placed[2, 1], placed[3, 0]
    plus0[...], minus1[...] = placed[1, 0], placed[3, 1]


def add_kernel(plus0, left, minus1, right, to_right, to_left):
    to_right[...] = (plus0[...].astype(F32) + left[0].astype(F32)).astype(BF16)
    to_left[...] = (minus1[...].astype(F32) + right[0].astype(F32)).astype(BF16)


def total_kernel(here, left, right, left0, right1, keep, across, near, cross):
    own = here[0].astype(F32) + left0[...].astype(F32) + right[1].astype(F32)
    keep[...] = own[0]
    across[...] = own[1].astype(BF16)
    other = here[1].astype(F32) + left[1].astype(F32) + right1[...].astype(F32)
    near[...] = other[0].astype(BF16)
    cross[...] = other[1].astype(BF16)


def finish_kernel(meta, base, keep, across, near, cross, out):
    y_lo, start = meta[1], (meta[3] * 2 + meta[4]) * 1024
    mine, other = y_lo * 512, (1 - y_lo) * 512
    out[:, aligned(mine, 512)] = (
        base[:, aligned(start + mine, 512)].astype(F32) + (keep[...] + across[...].astype(F32))
    ).astype(BF16)
    out[:, aligned(other, 512)] = (
        base[:, aligned(start + other, 512)].astype(F32)
        + (near[...].astype(F32) + cross[...].astype(F32))
    ).astype(BF16)


def summed(meta, own, arrived, w, found, base):
    keys = [(s, w, c) for s in range(Z) for c in range(2)]
    arrays = [found[key][0] for key in keys]
    specs = [one_block(*found[key]) for key in keys]
    part, pair = shape(2, 128, 512), shape(2, 2, 128, 512)
    right, left, plus0, minus1, here = call(
        functools.partial(expand_kernel, keys, 1 - w),
        [pair, pair, part, part, pair],
        [meta, own, arrived] + arrays,
        [SMEM, VMEM, VMEM] + specs,
        flops=2 * 256 * 512 * 4096,
        scratch=[pltpu.VMEM((4, 2, 2, 128, 512), BF16)],
        grid=(1,),
    )
    left, right = along_x(right, 1), along_x(left, -1)
    plus0, minus1 = call(add_kernel, [part] * 2, [plus0, left, minus1, right], [VMEM] * 4)
    left0, right1 = along_x(plus0, 1), along_x(minus1, -1)
    flat = shape(128, 512)
    keep, across, near, cross = call(
        total_kernel,
        [shape(128, 512, kind=F32), flat, flat, flat],
        [here, left, right, left0, right1],
        [VMEM] * 5,
    )
    across, near, cross = swap_far_y(across), swap_y(near), swap_other_y(cross)
    return call(finish_kernel, [shape(128, 1024)], [meta, base, keep, across, near, cross])[0]


def shards(hidden, encodings, span_slot, w_query, w_out, w_keyval, grad_out):
    batch = lax.axis_index("batch")
    tensor = lax.axis_index("tensor")
    meta = jnp.stack([batch >> 2, (batch >> 1) & 1, batch & 1, tensor >> 1, tensor & 1]).astype(jnp.int32)

    own = jnp.stack([w_query, w_out])
    blocks = {0: own}
    blocks[1], blocks[7] = along_both(own, own)
    spread = call(spread_kernel, [shape(32, 2, 16, 128)], [encodings], [VMEM])[0]
    spread = lax.all_to_all(spread, "batch", 0, 0).reshape(64, 16, 128)
    halves = call(half_kernel, [shape(Z, 128, 512)] * 2, [after(meta, spread), hidden, grad_out])
    acts = [hidden, grad_out, swap_y(halves[0]), swap_other_y(halves[1])]
    chosen = call(choose_kernel, [shape(32, 2, 16, 128)], [span_slot, spread])[0]
    blocks[2], blocks[6] = along_both(after(blocks[1], chosen, *halves), after(blocks[7], chosen, *halves))
    chosen = lax.all_to_all(after(chosen, blocks[1], blocks[7], *halves), "batch", 0, 0)
    enc = call(assemble_kernel, [shape(512, 256)], [chosen], [VMEM])[0]
    blocks[3], blocks[5] = along_both(after(blocks[2], enc, *acts[2:]), after(blocks[6], enc, *acts[2:]))
    pieces = gather_features(after(enc, blocks[2], blocks[6]))
    ahead, back = after((blocks[3], blocks[5]), *[piece for _, _, piece in pieces[1:5]])
    last = [along_z(ahead[0], -1), along_z(back[1], 1)]
    found = with_core(blocks, last)
    keys, values = call(
        functools.partial(keyval_kernel, [(dx, dy) for dx, dy, _ in pieces]),
        [shape(512, 512)] * 2,
        [meta, w_keyval] + [piece for _, _, piece in pieces],
        flops=4 * 512 * 2048 * 512,
    )
    early = project((0, 1, 7, 2, 6), meta, acts, found)[0]
    own, sent = project((3, 5, 4), meta, acts, found, after(early, keys, values), True)
    rows = call(
        attend_kernel,
        [shape(2, 128, 512)],
        [own, swap_y(sent), keys, values],
        [VMEM] * 4,
        flops=10 * 8 * 64 * 256 * 128,
    )[0]
    arrived = swap_y(rows)
    layer_out = summed(meta, rows, arrived, 1, found, hidden)
    grad_hidden = summed(meta, rows, arrived, 0, found, grad_out)
    return (layer_out, grad_hidden)


def solution(mesh):
    return jax.shard_map(
        shards,
        mesh=mesh,
        in_specs=(
            P("batch", None),
            P("batch", "tensor"),
            P(),
            P("batch", "tensor"),
            P("batch", "tensor"),
            P(None, None, "tensor"),
            P("batch", None),
        ),
        out_specs=(P("batch", "tensor"), P("batch", "tensor")),
        check_vma=False,
    )
```

```python
import functools
import math

import jax
import jax.numpy as jnp
from jax import lax
from jax.experimental import pallas as pl
from jax.experimental.pallas import tpu as pltpu
from jax.sharding import PartitionSpec as P

HEAD = 128
CL = 64
NR = 256
Z = 8
BF16 = jnp.bfloat16
F32 = jnp.float32
MIB = 1 << 20


def along_z(a, step):
    return lax.ppermute(a, "batch", [(i, (i + 4 * step) % 32) for i in range(32)])


def swap_core(a):
    return lax.ppermute(a, "batch", [(i, i ^ 1) for i in range(32)])


def swap_y(a):
    return lax.ppermute(a, "batch", [(i, i ^ 2) for i in range(32)])


def swap_far_y(a):
    return lax.ppermute(a, "tensor", [(i, i ^ 1) for i in range(8)])


def swap_other_y(a):
    pairs = [(b * 8 + t, (b ^ 2) * 8 + (t ^ 1)) for b in range(32) for t in range(8)]
    return lax.ppermute(a, ("batch", "tensor"), pairs)


def along_x(a, step):
    return lax.ppermute(a, "tensor", [(i, (i + 2 * step) % 8) for i in range(8)])


def dot(a, b):
    return jnp.dot(a, b, preferred_element_type=F32)


def dot_t(a, b):
    return lax.dot_general(a, b, (((1,), (1,)), ((), ())), preferred_element_type=F32)


SMEM = pl.BlockSpec(memory_space=pltpu.SMEM)
VMEM = pl.BlockSpec(memory_space=pltpu.VMEM)


def call(kernel, outs, ins, specs=None, flops=0, limit=6, scratch=(), grid=()):
    size = sum(math.prod(a.shape) * a.dtype.itemsize for a in list(ins) + list(outs))
    return pl.pallas_call(
        kernel,
        out_shape=outs,
        in_specs=specs or [SMEM] + [VMEM] * (len(ins) - 1),
        out_specs=[VMEM] * len(outs),
        scratch_shapes=list(scratch),
        grid=grid,
        compiler_params=pltpu.CompilerParams(vmem_limit_bytes=limit * MIB),
        cost_estimate=pl.CostEstimate(flops=flops, bytes_accessed=size, transcendentals=0),
    )(*ins)


def shape(*dims, kind=BF16):
    return jax.ShapeDtypeStruct(dims, kind)


def aligned(offset, size):
    return pl.ds(pl.multiple_of(offset, size), size)


def spread_kernel(enc, out):
    for slot in range(2):
        for rows in range(16):
            for cols in range(2):
                out[rows * 2 + cols, slot] = enc[
                    slot * NR + rows * 16 : slot * NR + rows * 16 + 16,
                    cols * 128 : cols * 128 + 128,
                ]


def choose_kernel(slots, pieces, out):
    for span in range(64):
        out[span // 2, span % 2] = pieces[slots[span]]


def assemble_kernel(pieces, out):
    for span in range(2):
        for rows in range(16):
            for cols in range(2):
                out[
                    span * NR + rows * 16 : span * NR + rows * 16 + 16,
                    cols * 128 : cols * 128 + 128,
                ] = pieces[rows * 2 + cols, span]


def keyval_kernel(places, meta, w, *refs):
    pieces, (keys, values) = refs[:-2], refs[-2:]
    x, y_hi = meta[3], meta[4]
    for kind, out in ((0, keys), (1, values)):
        total = None
        for (dx, dy), piece in zip(places, pieces):
            source = ((x - dx) & 3) * 2 + (y_hi ^ dy)
            term = dot(piece[...], w[kind, aligned(source * 256, 256), :])
            total = term if total is None else total + term
        out[...] = total.astype(BF16)


def half_kernel(meta, hidden, grad, out_hidden, out_grad):
    y_lo = meta[1]
    for source, out in ((hidden, out_hidden), (grad, out_grad)):
        for block in range(Z):
            out[block] = source[:, aligned(block * 1024 + (1 - y_lo) * 512, 512)]


def after(value, *others):
    return lax.optimization_barrier((value, others))[0]


def along_both(ahead, back):
    return along_z(ahead, -1), along_z(back, 1)


def with_core(blocks, last):
    found = {}
    behind = {0: 2, 1: 2, 7: 2, 2: 3, 6: 3}
    for step, block in blocks.items():
        if step in behind:
            ready = after(block, blocks[behind[step]], blocks[Z - behind[step]])
        else:
            ready = block
        theirs = swap_core(ready)
        for w in range(2):
            found[step, w, 0], found[step, w, 1] = (block, w), (theirs, w)
    for w in range(2):
        found[Z // 2, w, 0], found[Z // 2, w, 1] = (last[w], None), (swap_core(last[w]), None)
    return found


def one_block(array, index):
    if index is None:
        return pl.BlockSpec(array.shape, lambda i: (0, 0))
    return pl.BlockSpec((None,) + array.shape[1:], lambda i: (index, 0, 0))


def project_kernel(keys, places, first, last, meta, hidden, grad, hidden_in, grad_in, *refs):
    z, y_lo, core = meta[0], meta[1], meta[2]
    refs = list(refs)
    before = None if first else refs.pop(0)
    outs = refs[len(refs) - 1 - last :]
    for w, (own, arrived) in enumerate(((hidden, hidden_in), (grad, grad_in))):
        total = None if first else before[w]
        for step, kind, apart in keys:
            if kind != w:
                continue
            place, side = (z + step) & 7, core ^ apart
            left = jnp.concatenate(
                [
                    own[:, aligned(place * 1024 + y_lo * 512 + side * 256, 256)],
                    arrived[place, :, aligned(side * 256, 256)],
                ],
                axis=0,
            )
            number, index = places[step, kind, apart]
            block = refs[number][...] if index is None else refs[number][index]
            term = dot(left, block)
            total = term if total is None else total + term
        if last:
            outs[0][w] = total[:128]
            outs[1][w] = total[128:].astype(BF16)
        else:
            outs[0][w] = total


def project(steps, meta, acts, found, before=None, last=False):
    keys = [(s, w, c) for s in steps for w in range(2) for c in range(2)]
    arrays, places = [], {}
    for key in keys:
        array, index = found[key]
        number = next((n for n, a in enumerate(arrays) if a is array), len(arrays))
        if number == len(arrays):
            arrays.append(array)
        places[key] = (number, index)
    ins = [meta, *acts] + ([] if before is None else [before]) + arrays
    if last:
        outs = [shape(2, 128, 512, kind=F32), shape(2, 128, 512)]
    else:
        outs = [shape(2, 256, 512, kind=F32)]
    kernel = functools.partial(project_kernel, keys, places, before is None, last)
    return call(kernel, outs, ins, flops=len(keys) * 2 * 256 * 256 * 512, limit=20)


def attend_kernel(own, arrived, keys, values, both):
    scaling = 1.0 / math.sqrt(HEAD)
    query = ((own[0] + arrived[0].astype(F32)) * scaling).astype(BF16)
    grad = (own[1] + arrived[1].astype(F32)).astype(BF16)
    for span in range(2):
        rows = slice(span * CL, span * CL + CL)
        for head in range(4):
            cols = slice(head * HEAD, head * HEAD + HEAD)
            k = keys[span * NR : span * NR + NR, cols]
            v = values[span * NR : span * NR + NR, cols]
            scores = dot_t(query[rows, cols], k)
            top = jnp.max(scores, axis=-1, keepdims=True)
            powers = jnp.exp(scores - top)
            probs = powers / jnp.sum(powers, axis=-1, keepdims=True)
            out = dot(probs.astype(BF16), v).astype(BF16)
            both[0, rows, cols] = out
            g = grad[rows, cols]
            delta = jnp.sum(g.astype(F32) * out.astype(F32), axis=-1, keepdims=True)
            grad_scores = (probs * (dot_t(g, v) - delta)).astype(BF16)
            both[1, rows, cols] = (dot(grad_scores, k) * scaling).astype(BF16)


def expand_kernel(keys, kind, meta, rows, *refs):
    z, core, x, y_hi = meta[0], meta[2], meta[3], meta[4]
    blocks = refs[: len(keys)]
    *outs, placed = refs[len(keys) :]
    left = rows[kind]
    for (step, _, apart), block in zip(keys, blocks):
        target = (z + step) & 7
        dx, dy = ((target >> 1) - x) & 3, (target & 1) ^ y_hi
        part = dot_t(left, block[...]).astype(BF16)
        placed[dx, dy, :, aligned((core ^ apart) * 256, 256)] = part
    for dx, out in enumerate(outs):
        out[...] = placed[dx]


def add_kernel(plus0, far0, minus1, far1, to_right, to_left):
    to_right[...] = (plus0[...].astype(F32) + far0[...].astype(F32)).astype(BF16)
    to_left[...] = (minus1[...].astype(F32) + far1[...].astype(F32)).astype(BF16)


def total_kernel(here0, here1, left0, left1, right0, right1, keep, across, near, cross):
    own = here0[...].astype(F32) + left0[...].astype(F32) + right0[...].astype(F32)
    keep[...] = own[0]
    across[...] = own[1].astype(BF16)
    other = here1[...].astype(F32) + left1[...].astype(F32) + right1[...].astype(F32)
    near[...] = other[0].astype(BF16)
    cross[...] = other[1].astype(BF16)


def finish_kernel(meta, base, keep, across, near, cross, out):
    y_lo, start = meta[1], (meta[3] * 2 + meta[4]) * 1024
    mine, other = y_lo * 512, (1 - y_lo) * 512
    out[:, aligned(mine, 512)] = (
        base[:, aligned(start + mine, 512)].astype(F32) + (keep[...] + across[...].astype(F32))
    ).astype(BF16)
    out[:, aligned(other, 512)] = (
        base[:, aligned(start + other, 512)].astype(F32)
        + (near[...].astype(F32) + cross[...].astype(F32))
    ).astype(BF16)


def expand(meta, rows, w, found):
    keys = [(s, w, c) for s in range(Z) for c in range(2)]
    part = shape(2, 128, 512)
    return call(
        functools.partial(expand_kernel, keys, 1 - w),
        [part] * 4,
        [meta, rows] + [found[key][0] for key in keys],
        [SMEM, VMEM] + [one_block(*found[key]) for key in keys],
        flops=2 * 128 * 512 * 4096,
        limit=20,
        scratch=[pltpu.VMEM((4, 2, 128, 512), BF16)],
        grid=(1,),
    )


def send_own(parts):
    return along_x(parts[2], 1), along_x(parts[3], -1)


def summed(meta, own, sent, parts, base):
    part = shape(2, 128, 512)
    far0, right0 = sent
    far1, left1 = along_x(parts[2], -1), along_x(parts[1], 1)
    plus0, minus1 = call(add_kernel, [part] * 2, [own[1], far0, parts[3], far1], [VMEM] * 4)
    left0, right1 = along_x(plus0, 1), along_x(minus1, -1)
    flat = shape(128, 512)
    keep, across, near, cross = call(
        total_kernel,
        [shape(128, 512, kind=F32), flat, flat, flat],
        [own[0], parts[0], left0, left1, right0, right1],
        [VMEM] * 6,
    )
    across, near, cross = swap_far_y(across), swap_y(near), swap_other_y(cross)
    return call(finish_kernel, [shape(128, 1024)], [meta, base, keep, across, near, cross], limit=8)[0]


def shards(hidden, encodings, span_slot, w_query, w_out, w_keyval, grad_out):
    batch = lax.axis_index("batch")
    tensor = lax.axis_index("tensor")
    meta = jnp.stack([batch >> 2, (batch >> 1) & 1, batch & 1, tensor >> 1, tensor & 1]).astype(jnp.int32)

    own = jnp.stack([w_query, w_out])
    blocks = {0: own}
    blocks[1], blocks[7] = along_both(own, own)
    spread = call(spread_kernel, [shape(32, 2, 16, 128)], [encodings], [VMEM])[0]
    spread = lax.all_to_all(spread, "batch", 0, 0).reshape(64, 16, 128)
    halves = call(half_kernel, [shape(Z, 128, 512)] * 2, [after(meta, spread), hidden, grad_out], limit=10)
    acts = [hidden, grad_out, swap_y(halves[0]), swap_other_y(halves[1])]
    chosen = call(choose_kernel, [shape(32, 2, 16, 128)], [span_slot, spread])[0]
    blocks[2], blocks[6] = along_both(after(blocks[1], chosen, *halves), after(blocks[7], chosen, *halves))
    chosen = lax.all_to_all(after(chosen, blocks[1], blocks[7], *halves), "batch", 0, 0)
    enc = call(assemble_kernel, [shape(512, 256)], [chosen], [VMEM])[0]
    blocks[3], blocks[5] = along_both(after(blocks[2], enc, *acts[2:]), after(blocks[6], enc, *acts[2:]))
    enc = after(enc, blocks[2], blocks[6])
    other = swap_far_y(enc)
    near = (other, along_x(enc, 1), along_x(enc, -1), blocks[3], blocks[5])
    enc_far, other_near = after((enc, other), *near)
    pieces = [(0, 0, enc), (0, 1, other), (1, 0, near[1]), (-1, 0, near[2]), (2, 0, along_x(enc_far, 2))]
    pieces += [(1, 1, along_x(other_near, 1)), (-1, 1, along_x(other_near, -1))]
    ahead, back = after((blocks[3], blocks[5]), *near)
    last = [along_z(ahead[0], -1), along_z(back[1], 1)]
    pieces.append((2, 1, along_x(after(other, *last, *[piece for _, _, piece in pieces[4:]]), 2)))
    found = with_core(blocks, last)
    keys, values = call(
        functools.partial(keyval_kernel, [(dx, dy) for dx, dy, _ in pieces]),
        [shape(512, 512)] * 2,
        [meta, w_keyval] + [piece for _, _, piece in pieces],
        flops=4 * 512 * 2048 * 512,
        limit=16,
    )
    early = project((0, 1, 7, 2, 6), meta, acts, found)[0]
    own, sent = project((3, 5, 4), meta, acts, found, early, True)
    rows = call(
        attend_kernel,
        [shape(2, 128, 512)],
        [own, swap_y(sent), keys, values],
        [VMEM] * 4,
        flops=10 * 8 * 64 * 256 * 128,
    )[0]
    arrived = swap_y(rows)
    own = [expand(meta, rows, w, found) for w in (1, 0)]
    sent = [send_own(parts) for parts in own]
    parts = [expand(meta, after(arrived, *sent[n]), w, found) for n, w in enumerate((1, 0))]
    layer_out = summed(meta, own[0], sent[0], parts[0], hidden)
    grad_hidden = summed(meta, own[1], sent[1], parts[1], grad_out)
    return (layer_out, grad_hidden)


def solution(mesh):
    return jax.shard_map(
        shards,
        mesh=mesh,
        in_specs=(
            P("batch", None),
            P("batch", "tensor"),
            P(),
            P("batch", "tensor"),
            P("batch", "tensor"),
            P(None, None, "tensor"),
            P("batch", None),
        ),
        out_specs=(P("batch", "tensor"), P("batch", "tensor")),
        check_vma=False,
    )
```

```python
import functools
import math

import jax
import jax.numpy as jnp
from jax import lax
from jax.experimental import pallas as pl
from jax.experimental.pallas import tpu as pltpu
from jax.sharding import PartitionSpec as P

HEAD = 128
CL = 64
NR = 256
Z = 8
BF16 = jnp.bfloat16
F32 = jnp.float32
MIB = 1 << 20


def along_z(a, step):
    return lax.ppermute(a, "batch", [(i, (i + 4 * step) % 32) for i in range(32)])


def swap_core(a):
    return lax.ppermute(a, "batch", [(i, i ^ 1) for i in range(32)])


def swap_y(a):
    return lax.ppermute(a, "batch", [(i, i ^ 2) for i in range(32)])


def swap_far_y(a):
    return lax.ppermute(a, "tensor", [(i, i ^ 1) for i in range(8)])


def swap_other_y(a):
    pairs = [(b * 8 + t, (b ^ 2) * 8 + (t ^ 1)) for b in range(32) for t in range(8)]
    return lax.ppermute(a, ("batch", "tensor"), pairs)


def along_x(a, step):
    return lax.ppermute(a, "tensor", [(i, (i + 2 * step) % 8) for i in range(8)])


def dot(a, b):
    return jnp.dot(a, b, preferred_element_type=F32)


def dot_t(a, b):
    return lax.dot_general(a, b, (((1,), (1,)), ((), ())), preferred_element_type=F32)


SMEM = pl.BlockSpec(memory_space=pltpu.SMEM)
VMEM = pl.BlockSpec(memory_space=pltpu.VMEM)


def call(kernel, outs, ins, specs=None, flops=0, limit=6, scratch=(), grid=()):
    size = sum(math.prod(a.shape) * a.dtype.itemsize for a in list(ins) + list(outs))
    return pl.pallas_call(
        kernel,
        out_shape=outs,
        in_specs=specs or [SMEM] + [VMEM] * (len(ins) - 1),
        out_specs=[VMEM] * len(outs),
        scratch_shapes=list(scratch),
        grid=grid,
        compiler_params=pltpu.CompilerParams(vmem_limit_bytes=limit * MIB),
        cost_estimate=pl.CostEstimate(flops=flops, bytes_accessed=size, transcendentals=0),
    )(*ins)


def shape(*dims, kind=BF16):
    return jax.ShapeDtypeStruct(dims, kind)


def aligned(offset, size):
    return pl.ds(pl.multiple_of(offset, size), size)


def spread_kernel(enc, out):
    for slot in range(2):
        for rows in range(16):
            for cols in range(2):
                out[rows * 2 + cols, slot] = enc[
                    slot * NR + rows * 16 : slot * NR + rows * 16 + 16,
                    cols * 128 : cols * 128 + 128,
                ]


def choose_kernel(slots, pieces, out):
    for span in range(64):
        out[span // 2, span % 2] = pieces[slots[span]]


def assemble_kernel(pieces, out):
    for span in range(2):
        for rows in range(16):
            for cols in range(2):
                out[
                    span * NR + rows * 16 : span * NR + rows * 16 + 16,
                    cols * 128 : cols * 128 + 128,
                ] = pieces[rows * 2 + cols, span]


def keyval_kernel(places, meta, w, *refs):
    pieces, (keys, values) = refs[:-2], refs[-2:]
    x, y_hi = meta[3], meta[4]
    for kind, out in ((0, keys), (1, values)):
        total = None
        for (dx, dy), piece in zip(places, pieces):
            source = ((x - dx) & 3) * 2 + (y_hi ^ dy)
            term = dot(piece[...], w[kind, aligned(source * 256, 256), :])
            total = term if total is None else total + term
        out[...] = total.astype(BF16)


def half_kernel(meta, hidden, grad, out_hidden, out_grad):
    y_lo = meta[1]
    for source, out in ((hidden, out_hidden), (grad, out_grad)):
        for block in range(Z):
            out[block] = source[:, aligned(block * 1024 + (1 - y_lo) * 512, 512)]


def after(value, *others):
    return lax.optimization_barrier((value, others))[0]


def along_both(ahead, back):
    return along_z(ahead, -1), along_z(back, 1)


def with_core(blocks, last):
    found = {}
    behind = {0: 2, 1: 2, 7: 2, 2: 3, 6: 3}
    for step, block in blocks.items():
        if step in behind:
            ready = after(block, blocks[behind[step]], blocks[Z - behind[step]])
        else:
            ready = block
        theirs = swap_core(ready)
        for w in range(2):
            found[step, w, 0], found[step, w, 1] = (block, w), (theirs, w)
    for w in range(2):
        found[Z // 2, w, 0], found[Z // 2, w, 1] = (last[w], None), (swap_core(last[w]), None)
    return found


def one_block(array, index):
    if index is None:
        return pl.BlockSpec(array.shape, lambda i: (0, 0))
    return pl.BlockSpec((None,) + array.shape[1:], lambda i: (index, 0, 0))


def project_kernel(keys, places, first, last, meta, hidden, grad, hidden_in, grad_in, *refs):
    z, y_lo, core = meta[0], meta[1], meta[2]
    refs = list(refs)
    before = None if first else refs.pop(0)
    outs = refs[len(refs) - 1 - last :]
    for w, (own, arrived) in enumerate(((hidden, hidden_in), (grad, grad_in))):
        total = None if first else before[w]
        for step, kind, apart in keys:
            if kind != w:
                continue
            place, side = (z + step) & 7, core ^ apart
            left = jnp.concatenate(
                [
                    own[:, aligned(place * 1024 + y_lo * 512 + side * 256, 256)],
                    arrived[place, :, aligned(side * 256, 256)],
                ],
                axis=0,
            )
            number, index = places[step, kind, apart]
            block = refs[number][...] if index is None else refs[number][index]
            term = dot(left, block)
            total = term if total is None else total + term
        if last:
            outs[0][w] = total[:128]
            outs[1][w] = total[128:].astype(BF16)
        else:
            outs[0][w] = total


def project(steps, meta, acts, found, before=None, last=False):
    keys = [(s, w, c) for s in steps for w in range(2) for c in range(2)]
    arrays, places = [], {}
    for key in keys:
        array, index = found[key]
        number = next((n for n, a in enumerate(arrays) if a is array), len(arrays))
        if number == len(arrays):
            arrays.append(array)
        places[key] = (number, index)
    ins = [meta, *acts] + ([] if before is None else [before]) + arrays
    if last:
        outs = [shape(2, 128, 512, kind=F32), shape(2, 128, 512)]
    else:
        outs = [shape(2, 256, 512, kind=F32)]
    kernel = functools.partial(project_kernel, keys, places, before is None, last)
    return call(kernel, outs, ins, flops=len(keys) * 2 * 256 * 256 * 512, limit=20)


def attend_kernel(own, arrived, keys, values, both):
    scaling = 1.0 / math.sqrt(HEAD)
    query = ((own[0] + arrived[0].astype(F32)) * scaling).astype(BF16)
    grad = (own[1] + arrived[1].astype(F32)).astype(BF16)
    for span in range(2):
        rows = slice(span * CL, span * CL + CL)
        for head in range(4):
            cols = slice(head * HEAD, head * HEAD + HEAD)
            k = keys[span * NR : span * NR + NR, cols]
            v = values[span * NR : span * NR + NR, cols]
            scores = dot_t(query[rows, cols], k)
            top = jnp.max(scores, axis=-1, keepdims=True)
            powers = jnp.exp(scores - top)
            probs = powers / jnp.sum(powers, axis=-1, keepdims=True)
            out = dot(probs.astype(BF16), v).astype(BF16)
            both[0, rows, cols] = out
            g = grad[rows, cols]
            delta = jnp.sum(g.astype(F32) * out.astype(F32), axis=-1, keepdims=True)
            grad_scores = (probs * (dot_t(g, v) - delta)).astype(BF16)
            both[1, rows, cols] = (dot(grad_scores, k) * scaling).astype(BF16)


def expand_kernel(keys, kind, meta, rows, *refs):
    z, core, x, y_hi = meta[0], meta[2], meta[3], meta[4]
    blocks = refs[: len(keys)]
    *outs, placed = refs[len(keys) :]
    left = rows[kind]
    for (step, _, apart), block in zip(keys, blocks):
        target = (z + step) & 7
        dx, dy = ((target >> 1) - x) & 3, (target & 1) ^ y_hi
        part = dot_t(left, block[...]).astype(BF16)
        placed[dx, dy, :, aligned((core ^ apart) * 256, 256)] = part
    for dx, out in enumerate(outs):
        out[...] = placed[dx]


def add_kernel(here, arrived, out):
    out[...] = (here[...].astype(F32) + arrived[...].astype(F32)).astype(BF16)


def total_kernel(here0, here1, left0, left1, right0, right1, keep, across, near, cross):
    own = here0[...].astype(F32) + left0[...].astype(F32) + right0[...].astype(F32)
    keep[...] = own[0]
    across[...] = own[1].astype(BF16)
    other = here1[...].astype(F32) + left1[...].astype(F32) + right1[...].astype(F32)
    near[...] = other[0].astype(BF16)
    cross[...] = other[1].astype(BF16)


def finish_kernel(meta, base, keep, across, near, cross, out):
    y_lo, start = meta[1], (meta[3] * 2 + meta[4]) * 1024
    mine, other = y_lo * 512, (1 - y_lo) * 512
    out[:, aligned(mine, 512)] = (
        base[:, aligned(start + mine, 512)].astype(F32) + (keep[...] + across[...].astype(F32))
    ).astype(BF16)
    out[:, aligned(other, 512)] = (
        base[:, aligned(start + other, 512)].astype(F32)
        + (near[...].astype(F32) + cross[...].astype(F32))
    ).astype(BF16)


def expand(meta, rows, w, found):
    keys = [(s, w, c) for s in range(Z) for c in range(2)]
    part = shape(2, 128, 512)
    return call(
        functools.partial(expand_kernel, keys, 1 - w),
        [part] * 4,
        [meta, rows] + [found[key][0] for key in keys],
        [SMEM, VMEM] + [one_block(*found[key]) for key in keys],
        flops=2 * 128 * 512 * 4096,
        limit=20,
        scratch=[pltpu.VMEM((4, 2, 128, 512), BF16)],
        grid=(1,),
    )


def send_own(parts):
    far0, right0 = along_x(parts[2], 1), along_x(parts[3], -1)
    return far0, right0, along_x(call(add_kernel, [shape(2, 128, 512)], [parts[1], far0], [VMEM] * 2)[0], 1)


def summed(meta, own, sent, parts, base):
    part = shape(2, 128, 512)
    _, right0, left0 = sent
    far1, left1 = along_x(parts[2], -1), along_x(parts[1], 1)
    right1 = along_x(call(add_kernel, [part], [parts[3], far1], [VMEM] * 2)[0], -1)
    flat = shape(128, 512)
    keep, across, near, cross = call(
        total_kernel,
        [shape(128, 512, kind=F32), flat, flat, flat],
        [own[0], parts[0], left0, left1, right0, right1],
        [VMEM] * 6,
    )
    across, near, cross = swap_far_y(across), swap_y(near), swap_other_y(cross)
    return call(finish_kernel, [shape(128, 1024)], [meta, base, keep, across, near, cross], limit=8)[0]


def shards(hidden, encodings, span_slot, w_query, w_out, w_keyval, grad_out):
    batch = lax.axis_index("batch")
    tensor = lax.axis_index("tensor")
    meta = jnp.stack([batch >> 2, (batch >> 1) & 1, batch & 1, tensor >> 1, tensor & 1]).astype(jnp.int32)

    own = jnp.stack([w_query, w_out])
    blocks = {0: own}
    blocks[1], blocks[7] = along_both(own, own)
    spread = call(spread_kernel, [shape(32, 2, 16, 128)], [encodings], [VMEM])[0]
    spread = lax.all_to_all(spread, "batch", 0, 0).reshape(64, 16, 128)
    halves = call(half_kernel, [shape(Z, 128, 512)] * 2, [after(meta, spread), hidden, grad_out], limit=10)
    acts = [hidden, grad_out, swap_y(halves[0]), swap_other_y(halves[1])]
    chosen = call(choose_kernel, [shape(32, 2, 16, 128)], [span_slot, spread])[0]
    blocks[2], blocks[6] = along_both(after(blocks[1], chosen, *halves), after(blocks[7], chosen, *halves))
    chosen = lax.all_to_all(after(chosen, blocks[1], blocks[7], *halves), "batch", 0, 0)
    enc = call(assemble_kernel, [shape(512, 256)], [chosen], [VMEM])[0]
    blocks[3], blocks[5] = along_both(after(blocks[2], enc, *acts[2:]), after(blocks[6], enc, *acts[2:]))
    enc = after(enc, blocks[2], blocks[6])
    other = swap_far_y(enc)
    near = (other, along_x(enc, 1), along_x(enc, -1), blocks[3], blocks[5])
    enc_far, other_near = after((enc, other), *near)
    pieces = [(0, 0, enc), (0, 1, other), (1, 0, near[1]), (-1, 0, near[2]), (2, 0, along_x(enc_far, 2))]
    pieces += [(1, 1, along_x(other_near, 1)), (-1, 1, along_x(other_near, -1))]
    ahead, back = after((blocks[3], blocks[5]), *near)
    last = [along_z(ahead[0], -1), along_z(back[1], 1)]
    pieces.append((2, 1, along_x(after(other, *last, *[piece for _, _, piece in pieces[4:]]), 2)))
    found = with_core(blocks, last)
    keys, values = call(
        functools.partial(keyval_kernel, [(dx, dy) for dx, dy, _ in pieces]),
        [shape(512, 512)] * 2,
        [meta, w_keyval] + [piece for _, _, piece in pieces],
        flops=4 * 512 * 2048 * 512,
        limit=16,
    )
    early = project((0, 1, 7, 2, 6), meta, acts, found)[0]
    own, sent = project((3, 5, 4), meta, acts, found, early, True)
    rows = call(
        attend_kernel,
        [shape(2, 128, 512)],
        [own, swap_y(sent), keys, values],
        [VMEM] * 4,
        flops=10 * 8 * 64 * 256 * 128,
    )[0]
    arrived = swap_y(rows)
    own = [expand(meta, rows, w, found) for w in (1, 0)]
    sent = [send_own(parts) for parts in own]
    first = expand(meta, after(arrived, *sent[0][:2]), 1, found)
    parts = [first, expand(meta, after(arrived, *sent[1][:2], sent[0][2]), 0, found)]
    layer_out = summed(meta, own[0], sent[0], parts[0], hidden)
    grad_hidden = summed(meta, own[1], sent[1], parts[1], grad_out)
    return (layer_out, grad_hidden)


def solution(mesh):
    return jax.shard_map(
        shards,
        mesh=mesh,
        in_specs=(
            P("batch", None),
            P("batch", "tensor"),
            P(),
            P("batch", "tensor"),
            P("batch", "tensor"),
            P(None, None, "tensor"),
            P("batch", None),
        ),
        out_specs=(P("batch", "tensor"), P("batch", "tensor")),
        check_vma=False,
    )
```

```python
import functools
import math

import jax
import jax.numpy as jnp
from jax import lax
from jax.experimental import pallas as pl
from jax.experimental.pallas import tpu as pltpu
from jax.sharding import PartitionSpec as P

HEAD = 128
CL = 64
NR = 256
Z = 8
BF16 = jnp.bfloat16
F32 = jnp.float32
MIB = 1 << 20


def along_z(a, step):
    return lax.ppermute(a, "batch", [(i, (i + 4 * step) % 32) for i in range(32)])


def swap_core(a):
    return lax.ppermute(a, "batch", [(i, i ^ 1) for i in range(32)])


def swap_y(a):
    return lax.ppermute(a, "batch", [(i, i ^ 2) for i in range(32)])


def swap_far_y(a):
    return lax.ppermute(a, "tensor", [(i, i ^ 1) for i in range(8)])


def swap_other_y(a):
    pairs = [(b * 8 + t, (b ^ 2) * 8 + (t ^ 1)) for b in range(32) for t in range(8)]
    return lax.ppermute(a, ("batch", "tensor"), pairs)


def along_x(a, step):
    return lax.ppermute(a, "tensor", [(i, (i + 2 * step) % 8) for i in range(8)])


def dot(a, b):
    return jnp.dot(a, b, preferred_element_type=F32)


def dot_t(a, b):
    return lax.dot_general(a, b, (((1,), (1,)), ((), ())), preferred_element_type=F32)


SMEM = pl.BlockSpec(memory_space=pltpu.SMEM)
VMEM = pl.BlockSpec(memory_space=pltpu.VMEM)


def call(kernel, outs, ins, specs=None, flops=0, limit=6, scratch=(), grid=()):
    size = sum(math.prod(a.shape) * a.dtype.itemsize for a in list(ins) + list(outs))
    return pl.pallas_call(
        kernel,
        out_shape=outs,
        in_specs=specs or [SMEM] + [VMEM] * (len(ins) - 1),
        out_specs=[VMEM] * len(outs),
        scratch_shapes=list(scratch),
        grid=grid,
        compiler_params=pltpu.CompilerParams(vmem_limit_bytes=limit * MIB),
        cost_estimate=pl.CostEstimate(flops=flops, bytes_accessed=size, transcendentals=0),
    )(*ins)


def shape(*dims, kind=BF16):
    return jax.ShapeDtypeStruct(dims, kind)


def aligned(offset, size):
    return pl.ds(pl.multiple_of(offset, size), size)


def spread_kernel(enc, out):
    for slot in range(2):
        for rows in range(16):
            for cols in range(2):
                out[rows * 2 + cols, slot] = enc[
                    slot * NR + rows * 16 : slot * NR + rows * 16 + 16,
                    cols * 128 : cols * 128 + 128,
                ]


def choose_kernel(slots, pieces, out):
    for span in range(64):
        out[span // 2, span % 2] = pieces[slots[span]]


def assemble_kernel(pieces, out):
    for span in range(2):
        for rows in range(16):
            for cols in range(2):
                out[
                    span * NR + rows * 16 : span * NR + rows * 16 + 16,
                    cols * 128 : cols * 128 + 128,
                ] = pieces[rows * 2 + cols, span]


def keyval_kernel(places, meta, w, *refs):
    pieces, out = refs[:-1], refs[-1]
    x, y_hi = meta[3], meta[4]

    @pl.loop(0, 2)
    def _(kind):
        total = None
        for (dx, dy), piece in zip(places, pieces):
            source = ((x - dx) & 3) * 2 + (y_hi ^ dy)
            term = dot(piece[...], w[kind, aligned(source * 256, 256), :])
            total = term if total is None else total + term
        out[kind] = total.astype(BF16)


def half_kernel(meta, hidden, grad, out_hidden, out_grad):
    y_lo = meta[1]
    for source, out in ((hidden, out_hidden), (grad, out_grad)):


        @pl.loop(0, Z)
        def _(block, source=source, out=out):
            out[block] = source[:, aligned(block * 1024 + (1 - y_lo) * 512, 512)]


def after(value, *others):
    return lax.optimization_barrier((value, others))[0]


def along_both(ahead, back):
    return along_z(ahead, -1), along_z(back, 1)


def with_core(blocks, last):
    found = {}
    behind = {0: 2, 1: 2, 7: 2, 2: 3, 6: 3}
    for step, block in blocks.items():
        if step in behind:
            ready = after(block, blocks[behind[step]], blocks[Z - behind[step]])
        else:
            ready = block
        theirs = swap_core(ready)
        for w in range(2):
            found[step, w, 0], found[step, w, 1] = (block, w), (theirs, w)
    for w in range(2):
        found[Z // 2, w, 0], found[Z // 2, w, 1] = (last[w], None), (swap_core(last[w]), None)
    return found


def one_block(array, index):
    if index is None:
        return pl.BlockSpec(array.shape, lambda i: (0, 0))
    return pl.BlockSpec((None,) + array.shape[1:], lambda i: (index, 0, 0))


def project_kernel(keys, places, first, last, meta, hidden, grad, hidden_in, grad_in, *refs):
    z, y_lo, core = meta[0], meta[1], meta[2]
    refs = list(refs)
    before = None if first else refs.pop(0)
    outs = refs[len(refs) - 1 - last :]
    for w, (own, arrived) in enumerate(((hidden, hidden_in), (grad, grad_in))):
        total = None if first else before[w]
        for step, kind, apart in keys:
            if kind != w:
                continue
            place, side = (z + step) & 7, core ^ apart
            left = jnp.concatenate(
                [
                    own[:, aligned(place * 1024 + y_lo * 512 + side * 256, 256)],
                    arrived[place, :, aligned(side * 256, 256)],
                ],
                axis=0,
            )
            number, index = places[step, kind, apart]
            block = refs[number][...] if index is None else refs[number][index]
            term = dot(left, block)
            total = term if total is None else total + term
        if last:
            outs[0][w] = total[:128]
            outs[1][w] = total[128:].astype(BF16)
        else:
            outs[0][w] = total


def project(steps, meta, acts, found, before=None, last=False):
    keys = [(s, w, c) for s in steps for w in range(2) for c in range(2)]
    arrays, places = [], {}
    for key in keys:
        array, index = found[key]
        number = next((n for n, a in enumerate(arrays) if a is array), len(arrays))
        if number == len(arrays):
            arrays.append(array)
        places[key] = (number, index)
    ins = [meta, *acts] + ([] if before is None else [before]) + arrays
    if last:
        outs = [shape(2, 128, 512, kind=F32), shape(2, 128, 512)]
    else:
        outs = [shape(2, 256, 512, kind=F32)]
    kernel = functools.partial(project_kernel, keys, places, before is None, last)
    return call(kernel, outs, ins, flops=len(keys) * 2 * 256 * 256 * 512, limit=20)


def attend_kernel(own, arrived, keyval, both):
    scaling = 1.0 / math.sqrt(HEAD)

    @pl.loop(0, 2)
    def _(span):
        rows, long = aligned(span * CL, CL), aligned(span * NR, NR)
        query = ((own[0, rows, :] + arrived[0, rows, :].astype(F32)) * scaling).astype(BF16)
        grad = (own[1, rows, :] + arrived[1, rows, :].astype(F32)).astype(BF16)
        for head in range(4):
            cols = slice(head * HEAD, head * HEAD + HEAD)
            k, v = keyval[0, long, cols], keyval[1, long, cols]
            scores = dot_t(query[:, cols], k)
            top = jnp.max(scores, axis=-1, keepdims=True)
            powers = jnp.exp(scores - top)
            probs = powers / jnp.sum(powers, axis=-1, keepdims=True)
            out = dot(probs.astype(BF16), v).astype(BF16)
            both[0, rows, cols] = out
            g = grad[:, cols]
            delta = jnp.sum(g.astype(F32) * out.astype(F32), axis=-1, keepdims=True)
            grad_scores = (probs * (dot_t(g, v) - delta)).astype(BF16)
            both[1, rows, cols] = (dot(grad_scores, k) * scaling).astype(BF16)


def expand_kernel(keys, kind, meta, rows, *refs):
    z, core, x, y_hi = meta[0], meta[2], meta[3], meta[4]
    blocks = refs[: len(keys)]
    *outs, placed = refs[len(keys) :]
    left = rows[kind]
    for (step, _, apart), block in zip(keys, blocks):
        target = (z + step) & 7
        dx, dy = ((target >> 1) - x) & 3, (target & 1) ^ y_hi
        part = dot_t(left, block[...]).astype(BF16)
        placed[dx, dy, :, aligned((core ^ apart) * 256, 256)] = part
    for dx, out in enumerate(outs):
        out[...] = placed[dx]


def add_kernel(here, arrived, out):
    @pl.loop(0, 4)
    def _(part):
        rows = aligned(part * 32, 32)
        for dy in range(2):
            out[dy, rows, :] = (here[dy, rows, :].astype(F32) + arrived[dy, rows, :].astype(F32)).astype(BF16)


def total_kernel(here0, here1, left0, left1, right0, right1, keep, across, near, cross):
    @pl.loop(0, 4)
    def _(part):
        rows = aligned(part * 32, 32)
        own = [sum(a[dy, rows, :].astype(F32) for a in (here0, left0, right0)) for dy in range(2)]
        keep[rows, :] = own[0]
        across[rows, :] = own[1].astype(BF16)
        other = [sum(a[dy, rows, :].astype(F32) for a in (here1, left1, right1)) for dy in range(2)]
        near[rows, :] = other[0].astype(BF16)
        cross[rows, :] = other[1].astype(BF16)


def finish_kernel(meta, base, keep, across, near, cross, out):
    y_lo, start = meta[1], (meta[3] * 2 + meta[4]) * 1024
    mine, other = y_lo * 512, (1 - y_lo) * 512

    @pl.loop(0, 4)
    def _(part):
        rows = aligned(part * 32, 32)
        out[rows, aligned(mine, 512)] = (
            base[rows, aligned(start + mine, 512)].astype(F32)
            + (keep[rows, :] + across[rows, :].astype(F32))
        ).astype(BF16)
        out[rows, aligned(other, 512)] = (
            base[rows, aligned(start + other, 512)].astype(F32)
            + (near[rows, :].astype(F32) + cross[rows, :].astype(F32))
        ).astype(BF16)


def expand(meta, rows, w, found):
    keys = [(s, w, c) for s in range(Z) for c in range(2)]
    part = shape(2, 128, 512)
    return call(
        functools.partial(expand_kernel, keys, 1 - w),
        [part] * 4,
        [meta, rows] + [found[key][0] for key in keys],
        [SMEM, VMEM] + [one_block(*found[key]) for key in keys],
        flops=2 * 128 * 512 * 4096,
        limit=20,
        scratch=[pltpu.VMEM((4, 2, 128, 512), BF16)],
        grid=(1,),
    )


def send_own(parts):
    far0, right0 = along_x(parts[2], 1), along_x(parts[3], -1)
    return far0, right0, along_x(call(add_kernel, [shape(2, 128, 512)], [parts[1], far0], [VMEM] * 2)[0], 1)


def summed(meta, own, sent, parts, base):
    part = shape(2, 128, 512)
    _, right0, left0 = sent
    far1, left1 = along_x(parts[2], -1), along_x(parts[1], 1)
    right1 = along_x(call(add_kernel, [part], [parts[3], far1], [VMEM] * 2)[0], -1)
    flat = shape(128, 512)
    keep, across, near, cross = call(
        total_kernel,
        [shape(128, 512, kind=F32), flat, flat, flat],
        [own[0], parts[0], left0, left1, right0, right1],
        [VMEM] * 6,
    )
    across, near, cross = swap_far_y(across), swap_y(near), swap_other_y(cross)
    return call(finish_kernel, [shape(128, 1024)], [meta, base, keep, across, near, cross], limit=8)[0]


def shards(hidden, encodings, span_slot, w_query, w_out, w_keyval, grad_out):
    batch = lax.axis_index("batch")
    tensor = lax.axis_index("tensor")
    meta = jnp.stack([batch >> 2, (batch >> 1) & 1, batch & 1, tensor >> 1, tensor & 1]).astype(jnp.int32)

    own = jnp.stack([w_query, w_out])
    blocks = {0: own}
    blocks[1], blocks[7] = along_both(own, own)
    spread = call(spread_kernel, [shape(32, 2, 16, 128)], [encodings], [VMEM])[0]
    spread = lax.all_to_all(spread, "batch", 0, 0).reshape(64, 16, 128)
    halves = call(half_kernel, [shape(Z, 128, 512)] * 2, [after(meta, spread), hidden, grad_out], limit=10)
    acts = [hidden, grad_out, swap_y(halves[0]), swap_other_y(halves[1])]
    chosen = call(choose_kernel, [shape(32, 2, 16, 128)], [span_slot, spread])[0]
    blocks[2], blocks[6] = along_both(after(blocks[1], chosen, *halves), after(blocks[7], chosen, *halves))
    chosen = lax.all_to_all(after(chosen, blocks[1], blocks[7], *halves), "batch", 0, 0)
    enc = call(assemble_kernel, [shape(512, 256)], [chosen], [VMEM])[0]
    blocks[3], blocks[5] = along_both(after(blocks[2], enc, *acts[2:]), after(blocks[6], enc, *acts[2:]))
    enc = after(enc, blocks[2], blocks[6])
    other = swap_far_y(enc)
    near = (other, along_x(enc, 1), along_x(enc, -1), blocks[3], blocks[5])
    enc_far, other_near = after((enc, other), *near)
    pieces = [(0, 0, enc), (0, 1, other), (1, 0, near[1]), (-1, 0, near[2]), (2, 0, along_x(enc_far, 2))]
    pieces += [(1, 1, along_x(other_near, 1)), (-1, 1, along_x(other_near, -1))]
    ahead, back = after((blocks[3], blocks[5]), *near)
    last = [along_z(ahead[0], -1), along_z(back[1], 1)]
    pieces.append((2, 1, along_x(after(other, *last, *[piece for _, _, piece in pieces[4:]]), 2)))
    found = with_core(blocks, last)
    keyval = call(
        functools.partial(keyval_kernel, [(dx, dy) for dx, dy, _ in pieces]),
        [shape(2, 512, 512)],
        [meta, w_keyval] + [piece for _, _, piece in pieces],
        flops=4 * 512 * 2048 * 512,
        limit=16,
    )[0]
    early = project((0, 1, 7, 2, 6), meta, acts, found)[0]
    own, sent = project((3, 5, 4), meta, acts, found, early, True)
    rows = call(
        attend_kernel,
        [shape(2, 128, 512)],
        [own, swap_y(sent), keyval],
        [VMEM] * 3,
        flops=10 * 8 * 64 * 256 * 128,
    )[0]
    arrived = swap_y(rows)
    own = [expand(meta, rows, w, found) for w in (1, 0)]
    sent = [send_own(parts) for parts in own]
    first = expand(meta, after(arrived, *sent[0][:2]), 1, found)
    parts = [first, expand(meta, after(arrived, *sent[1][:2], sent[0][2]), 0, found)]
    layer_out = summed(meta, own[0], sent[0], parts[0], hidden)
    grad_hidden = summed(meta, own[1], sent[1], parts[1], grad_out)
    return (layer_out, grad_hidden)


def solution(mesh):
    return jax.shard_map(
        shards,
        mesh=mesh,
        in_specs=(
            P("batch", None),
            P("batch", "tensor"),
            P(),
            P("batch", "tensor"),
            P("batch", "tensor"),
            P(None, None, "tensor"),
            P("batch", None),
        ),
        out_specs=(P("batch", "tensor"), P("batch", "tensor")),
        check_vma=False,
    )
```

```python
import functools
import math

import jax
import jax.numpy as jnp
from jax import lax
from jax.experimental import pallas as pl
from jax.experimental.pallas import tpu as pltpu
from jax.sharding import PartitionSpec as P

HEAD = 128
CL = 64
NR = 256
Z = 8
BF16 = jnp.bfloat16
F32 = jnp.float32
MIB = 1 << 20


def along_z(a, step):
    return lax.ppermute(a, "batch", [(i, (i + 4 * step) % 32) for i in range(32)])


def swap_core(a):
    return lax.ppermute(a, "batch", [(i, i ^ 1) for i in range(32)])


def swap_y(a):
    return lax.ppermute(a, "batch", [(i, i ^ 2) for i in range(32)])


def swap_far_y(a):
    return lax.ppermute(a, "tensor", [(i, i ^ 1) for i in range(8)])


def swap_other_y(a):
    pairs = [(b * 8 + t, (b ^ 2) * 8 + (t ^ 1)) for b in range(32) for t in range(8)]
    return lax.ppermute(a, ("batch", "tensor"), pairs)


def along_x(a, step):
    return lax.ppermute(a, "tensor", [(i, (i + 2 * step) % 8) for i in range(8)])


def dot(a, b):
    return jnp.dot(a, b, preferred_element_type=F32)


def dot_t(a, b):
    return lax.dot_general(a, b, (((1,), (1,)), ((), ())), preferred_element_type=F32)


SMEM = pl.BlockSpec(memory_space=pltpu.SMEM)
VMEM = pl.BlockSpec(memory_space=pltpu.VMEM)


def call(kernel, outs, ins, specs=None, flops=0, limit=6, scratch=(), grid=()):
    size = sum(math.prod(a.shape) * a.dtype.itemsize for a in list(ins) + list(outs))
    return pl.pallas_call(
        kernel,
        out_shape=outs,
        in_specs=specs or [SMEM] + [VMEM] * (len(ins) - 1),
        out_specs=[VMEM] * len(outs),
        scratch_shapes=list(scratch),
        grid=grid,
        compiler_params=pltpu.CompilerParams(vmem_limit_bytes=limit * MIB),
        cost_estimate=pl.CostEstimate(flops=flops, bytes_accessed=size, transcendentals=0),
    )(*ins)


def shape(*dims, kind=BF16):
    return jax.ShapeDtypeStruct(dims, kind)


def aligned(offset, size):
    return pl.ds(pl.multiple_of(offset, size), size)


def spread_kernel(enc, out):
    for slot in range(2):
        for rows in range(16):
            for cols in range(2):
                out[rows * 2 + cols, slot] = enc[
                    slot * NR + rows * 16 : slot * NR + rows * 16 + 16,
                    cols * 128 : cols * 128 + 128,
                ]


def choose_kernel(slots, pieces, out):
    for span in range(64):
        out[span // 2, span % 2] = pieces[slots[span]]


def assemble_kernel(pieces, out):
    for span in range(2):
        for rows in range(16):
            for cols in range(2):
                out[
                    span * NR + rows * 16 : span * NR + rows * 16 + 16,
                    cols * 128 : cols * 128 + 128,
                ] = pieces[rows * 2 + cols, span]


def keyval_kernel(places, meta, w, *refs):
    pieces, out = refs[:-1], refs[-1]
    x, y_hi = meta[3], meta[4]

    @pl.loop(0, 2)
    def _(kind):
        total = None
        for (dx, dy), piece in zip(places, pieces):
            source = ((x - dx) & 3) * 2 + (y_hi ^ dy)
            term = dot(piece[...], w[kind, aligned(source * 256, 256), :])
            total = term if total is None else total + term
        out[kind] = total.astype(BF16)


def half_kernel(meta, hidden, grad, out_hidden, out_grad):
    y_lo = meta[1]
    for source, out in ((hidden, out_hidden), (grad, out_grad)):


        @pl.loop(0, Z)
        def _(block, source=source, out=out):
            out[block] = source[:, aligned(block * 1024 + (1 - y_lo) * 512, 512)]


def after(value, *others):
    return lax.optimization_barrier((value, others))[0]


def along_both(ahead, back):
    return along_z(ahead, -1), along_z(back, 1)


def with_core(blocks, last):
    found = {}
    behind = {0: 2, 1: 2, 7: 2, 2: 3, 6: 3}
    for step, block in blocks.items():
        if step in behind:
            ready = after(block, blocks[behind[step]], blocks[Z - behind[step]])
        else:
            ready = block
        theirs = swap_core(ready)
        for w in range(2):
            found[step, w, 0], found[step, w, 1] = (block, w), (theirs, w)
    for w in range(2):
        found[Z // 2, w, 0], found[Z // 2, w, 1] = (last[w], None), (swap_core(last[w]), None)
    return found


def one_block(array, index):
    if index is None:
        return pl.BlockSpec((array.shape[0] // 2, array.shape[1]), lambda i: (i, 0))
    return pl.BlockSpec((None, array.shape[1] // 2, array.shape[2]), lambda i: (index, i, 0))


def project_kernel(keys, places, first, last, meta, hidden, grad, hidden_in, grad_in, *refs):
    z, y_lo, core = meta[0], meta[1], meta[2]
    refs = list(refs)
    before = None if first else refs.pop(0)
    outs = refs[len(refs) - 1 - last :]
    for w, (own, arrived) in enumerate(((hidden, hidden_in), (grad, grad_in))):
        total = None if first else before[w]
        for step, kind, apart in keys:
            if kind != w:
                continue
            place, side = (z + step) & 7, core ^ apart
            left = jnp.concatenate(
                [
                    own[:, aligned(place * 1024 + y_lo * 512 + side * 256, 256)],
                    arrived[place, :, aligned(side * 256, 256)],
                ],
                axis=0,
            )
            number, index = places[step, kind, apart]
            block = refs[number][...] if index is None else refs[number][index]
            term = dot(left, block)
            total = term if total is None else total + term
        if last:
            outs[0][w] = total[:128]
            outs[1][w] = total[128:].astype(BF16)
        else:
            outs[0][w] = total


def project(steps, meta, acts, found, before=None, last=False):
    keys = [(s, w, c) for s in steps for w in range(2) for c in range(2)]
    arrays, places = [], {}
    for key in keys:
        array, index = found[key]
        number = next((n for n, a in enumerate(arrays) if a is array), len(arrays))
        if number == len(arrays):
            arrays.append(array)
        places[key] = (number, index)
    ins = [meta, *acts] + ([] if before is None else [before]) + arrays
    if last:
        outs = [shape(2, 128, 512, kind=F32), shape(2, 128, 512)]
    else:
        outs = [shape(2, 256, 512, kind=F32)]
    kernel = functools.partial(project_kernel, keys, places, before is None, last)
    return call(kernel, outs, ins, flops=len(keys) * 2 * 256 * 256 * 512, limit=20)


def attend_kernel(own, arrived, keyval, both):
    scaling = 1.0 / math.sqrt(HEAD)

    @pl.loop(0, 2)
    def _(span):
        rows, long = aligned(span * CL, CL), aligned(span * NR, NR)
        query = ((own[0, rows, :] + arrived[0, rows, :].astype(F32)) * scaling).astype(BF16)
        grad = (own[1, rows, :] + arrived[1, rows, :].astype(F32)).astype(BF16)
        for head in range(4):
            cols = slice(head * HEAD, head * HEAD + HEAD)
            k, v = keyval[0, long, cols], keyval[1, long, cols]
            scores = dot_t(query[:, cols], k)
            top = jnp.max(scores, axis=-1, keepdims=True)
            powers = jnp.exp(scores - top)
            probs = powers / jnp.sum(powers, axis=-1, keepdims=True)
            out = dot(probs.astype(BF16), v).astype(BF16)
            both[0, rows, cols] = out
            g = grad[:, cols]
            delta = jnp.sum(g.astype(F32) * out.astype(F32), axis=-1, keepdims=True)
            grad_scores = (probs * (dot_t(g, v) - delta)).astype(BF16)
            both[1, rows, cols] = (dot(grad_scores, k) * scaling).astype(BF16)


def expand_kernel(keys, kind, meta, rows, *refs):
    z, core, x, y_hi = meta[0], meta[2], meta[3], meta[4]
    blocks = refs[: len(keys)]
    *outs, placed = refs[len(keys) :]
    left = rows[kind]
    for (step, _, apart), block in zip(keys, blocks):
        target = (z + step) & 7
        dx, dy = ((target >> 1) - x) & 3, (target & 1) ^ y_hi
        part = dot_t(left, block[...]).astype(BF16)
        placed[dx, dy, :, aligned((core ^ apart) * 256 + pl.program_id(0) * 128, 128)] = part

    @pl.when(pl.program_id(0) == 1)
    def _():
        for dx, out in enumerate(outs):
            out[...] = placed[dx]


def add_kernel(here, arrived, out):
    @pl.loop(0, 4)
    def _(part):
        rows = aligned(part * 32, 32)
        for dy in range(2):
            out[dy, rows, :] = (here[dy, rows, :].astype(F32) + arrived[dy, rows, :].astype(F32)).astype(BF16)


def total_kernel(here0, here1, left0, left1, right0, right1, keep, across, near, cross):
    @pl.loop(0, 4)
    def _(part):
        rows = aligned(part * 32, 32)
        own = [sum(a[dy, rows, :].astype(F32) for a in (here0, left0, right0)) for dy in range(2)]
        keep[rows, :] = own[0]
        across[rows, :] = own[1].astype(BF16)
        other = [sum(a[dy, rows, :].astype(F32) for a in (here1, left1, right1)) for dy in range(2)]
        near[rows, :] = other[0].astype(BF16)
        cross[rows, :] = other[1].astype(BF16)


def finish_kernel(meta, base, keep, across, near, cross, out):
    y_lo, start = meta[1], (meta[3] * 2 + meta[4]) * 1024
    mine, other = y_lo * 512, (1 - y_lo) * 512

    @pl.loop(0, 4)
    def _(part):
        rows = aligned(part * 32, 32)
        out[rows, aligned(mine, 512)] = (
            base[rows, aligned(start + mine, 512)].astype(F32)
            + (keep[rows, :] + across[rows, :].astype(F32))
        ).astype(BF16)
        out[rows, aligned(other, 512)] = (
            base[rows, aligned(start + other, 512)].astype(F32)
            + (near[rows, :].astype(F32) + cross[rows, :].astype(F32))
        ).astype(BF16)


def expand(meta, rows, w, found):
    keys = [(s, w, c) for s in range(Z) for c in range(2)]
    part = shape(2, 128, 512)
    return call(
        functools.partial(expand_kernel, keys, 1 - w),
        [part] * 4,
        [meta, rows] + [found[key][0] for key in keys],
        [SMEM, VMEM] + [one_block(*found[key]) for key in keys],
        flops=2 * 128 * 512 * 4096,
        limit=20,
        scratch=[pltpu.VMEM((4, 2, 128, 512), BF16)],
        grid=(2,),
    )


def send_own(parts):
    far0, right0 = along_x(parts[2], 1), along_x(parts[3], -1)
    return far0, right0, along_x(call(add_kernel, [shape(2, 128, 512)], [parts[1], far0], [VMEM] * 2)[0], 1)


def summed(meta, own, sent, parts, base):
    part = shape(2, 128, 512)
    _, right0, left0 = sent
    far1, left1 = along_x(parts[2], -1), along_x(parts[1], 1)
    right1 = along_x(call(add_kernel, [part], [parts[3], far1], [VMEM] * 2)[0], -1)
    flat = shape(128, 512)
    keep, across, near, cross = call(
        total_kernel,
        [shape(128, 512, kind=F32), flat, flat, flat],
        [own[0], parts[0], left0, left1, right0, right1],
        [VMEM] * 6,
    )
    across, near, cross = swap_far_y(across), swap_y(near), swap_other_y(cross)
    return call(finish_kernel, [shape(128, 1024)], [meta, base, keep, across, near, cross], limit=8)[0]


def shards(hidden, encodings, span_slot, w_query, w_out, w_keyval, grad_out):
    batch = lax.axis_index("batch")
    tensor = lax.axis_index("tensor")
    meta = jnp.stack([batch >> 2, (batch >> 1) & 1, batch & 1, tensor >> 1, tensor & 1]).astype(jnp.int32)

    own = jnp.stack([w_query, w_out])
    blocks = {0: own}
    blocks[1], blocks[7] = along_both(own, own)
    spread = call(spread_kernel, [shape(32, 2, 16, 128)], [encodings], [VMEM])[0]
    spread = lax.all_to_all(spread, "batch", 0, 0).reshape(64, 16, 128)
    halves = call(half_kernel, [shape(Z, 128, 512)] * 2, [after(meta, spread), hidden, grad_out], limit=10)
    acts = [hidden, grad_out, swap_y(halves[0]), swap_other_y(halves[1])]
    chosen = call(choose_kernel, [shape(32, 2, 16, 128)], [span_slot, spread])[0]
    blocks[2], blocks[6] = along_both(after(blocks[1], chosen, *halves), after(blocks[7], chosen, *halves))
    chosen = lax.all_to_all(after(chosen, blocks[1], blocks[7], *halves), "batch", 0, 0)
    enc = call(assemble_kernel, [shape(512, 256)], [chosen], [VMEM])[0]
    blocks[3], blocks[5] = along_both(after(blocks[2], enc, *acts[2:]), after(blocks[6], enc, *acts[2:]))
    enc = after(enc, blocks[2], blocks[6])
    other = swap_far_y(enc)
    near = (other, along_x(enc, 1), along_x(enc, -1), blocks[3], blocks[5])
    enc_far, other_near = after((enc, other), *near)
    pieces = [(0, 0, enc), (0, 1, other), (1, 0, near[1]), (-1, 0, near[2]), (2, 0, along_x(enc_far, 2))]
    pieces += [(1, 1, along_x(other_near, 1)), (-1, 1, along_x(other_near, -1))]
    ahead, back = after((blocks[3], blocks[5]), *near)
    last = [along_z(ahead[0], -1), along_z(back[1], 1)]
    pieces.append((2, 1, along_x(after(other, *last, *[piece for _, _, piece in pieces[4:]]), 2)))
    found = with_core(blocks, last)
    keyval = call(
        functools.partial(keyval_kernel, [(dx, dy) for dx, dy, _ in pieces]),
        [shape(2, 512, 512)],
        [meta, w_keyval] + [piece for _, _, piece in pieces],
        flops=4 * 512 * 2048 * 512,
        limit=16,
    )[0]
    early = project((0, 1, 7, 2, 6), meta, acts, found)[0]
    own, sent = project((3, 5, 4), meta, acts, found, early, True)
    rows = call(
        attend_kernel,
        [shape(2, 128, 512)],
        [own, swap_y(sent), keyval],
        [VMEM] * 3,
        flops=10 * 8 * 64 * 256 * 128,
    )[0]
    arrived = swap_y(rows)
    own = [expand(meta, rows, w, found) for w in (1, 0)]
    sent = [send_own(parts) for parts in own]
    first = expand(meta, after(arrived, *sent[0][:2]), 1, found)
    parts = [first, expand(meta, after(arrived, *sent[1][:2], sent[0][2]), 0, found)]
    layer_out = summed(meta, own[0], sent[0], parts[0], hidden)
    grad_hidden = summed(meta, own[1], sent[1], parts[1], grad_out)
    return (layer_out, grad_hidden)


def solution(mesh):
    return jax.shard_map(
        shards,
        mesh=mesh,
        in_specs=(
            P("batch", None),
            P("batch", "tensor"),
            P(),
            P("batch", "tensor"),
            P("batch", "tensor"),
            P(None, None, "tensor"),
            P("batch", None),
        ),
        out_specs=(P("batch", "tensor"), P("batch", "tensor")),
        check_vma=False,
    )
```
